128 devices in a mesh: facet: 8 (over z, core), strip: 16 (over x, y).
Axes of the slice: x: 4, y: 4, z: 4, core: 2. Of those that a mesh axis runs over, the one named last changes fastest.
Arguments:
- sky_components: bfloat16 [8, 2, 4, 2048, 2048], P('facet', None, None, 'strip'), may hold values from -6 to 6
- scale_kernels: float32 [4, 33], replicated, may hold values from 0.026111647 to 0.26111647
- row_taper: bfloat16 [8, 2048, 1024], P('facet'), may hold values from -0.125 to 0.125
- col_taper: bfloat16 [8, 2048, 2048], P('facet'), may hold values from -0.125 to 0.125
- finish_rows: bfloat16 [8, 512, 128], replicated, may hold values from -0.1875 to 0.1875
- finish_cols: bfloat16 [8, 512, 128], replicated, may hold values from -0.5 to 0.5
- subgrid_owner: int32 [128], replicated, may hold values from 0 to 127, as said below
- block_cell: int32 [8192, 2], P(('facet', 'strip')), may hold values from 0 to 480
- vis_offset: float32 [8192, 2, 128], P(('facet', 'strip')), may hold values from 0 to 31
- block_owner: int32 [8192, 1], P(('facet', 'strip')), may hold values from 0 to 127; in each aligned block of 64 rows (0 to 63, 64 to 127, ...) at most 2 rows name the same one
- observed: float32 [32768, 2, 128], P(('facet', 'strip')), may hold values from -6 to 6
- antenna_pair_index: int32 [32768, 2, 128], P(('facet', 'strip')), may hold values from 0 to 511
- gains: float32 [2, 512], replicated, may hold values from 0.1 to 1.9
Outputs:
- subgrids: bfloat16 [128, 2, 512, 512], P(('facet', 'strip'))
- residual: float32 [32768, 2, 128], P(('facet', 'strip'))
The draws below stay inside these ranges and needn't reach their ends.
Inputs may be any that keep to these rules, and one draw needn't show every extreme that they name: Every device number appears once; subgrid_owner[a * 16 + b] = rowperm(a) * 16 + colperm(b) for a permutation rowperm of the subgrid rows and a permutation colperm of the subgrid columns. `block_owner`: among the 64 blocks of one device at most 2 share an owner, and some owner takes exactly 2 of them.
All inputs are finite; a program needn't handle non-finite values.
Results may differ from the reference program's by a relative error of at most 0.02.
Values may be sent and summed in bfloat16 or wider, within the bound.
No kernel may reach another device: no remote copies, remote signals or barrier semaphores. Data moves between devices by JAX's collectives and lax.ppermute only.
A program may use at most 128 MiB of HBM per device.

```python
import math
import jax
import jax.numpy as jnp
import numpy as np
from jax import lax

FS = 2048
CM = 128
SG = 512
TILE = 32
BLOCK_VISIBILITY = 128
CORRELATION_NUM = 2
SCALES = 4
HALF = 16
ANTENNA_COUNT = 512
BLK = 64
FACETS = 8
SUBROWS = 8
SUBCOLS = 16
SUBGRID_COUNT = 128
RECEIVE_BLOCKS = 2


def draw_subgrid_owner(key, part):
    row_perm = jax.random.permutation(jax.random.fold_in(key, 11), SUBROWS).astype(jnp.int32)
    col_perm = jax.random.permutation(jax.random.fold_in(key, 23), SUBCOLS).astype(jnp.int32)
    grid_ids = jnp.arange(SUBGRID_COUNT, dtype=jnp.int32)
    return (row_perm[grid_ids // SUBCOLS] * SUBCOLS + col_perm[grid_ids % SUBCOLS]).astype(jnp.int32)


def plant(array, own_key, low, largest):
    index_at = [jax.random.randint(jax.random.fold_in(own_key, axis), (), 0, length) for axis, length in enumerate(array.shape)]
    main_axis = array.shape.index(max(array.shape))
    neighbour = index_at[:main_axis] + [(index_at[main_axis] + 1) % array.shape[main_axis]] + index_at[main_axis + 1:]
    return array.at[tuple(index_at)].set(low).at[tuple(neighbour)].set(largest)


def block_scale(key, dims, split, smallest, top_value):
    level, own = 1.0, jax.random.fold_in(key, 6)
    for axis_at, shards_of in split:
        draws = jnp.exp(jax.random.uniform(jax.random.fold_in(own, axis_at), (shards_of,), jnp.float32, smallest / len(split), top_value / len(split)))
        level = level * jnp.repeat(draws, dims[axis_at] // shards_of).reshape([-1 if axis == axis_at else 1 for axis in range(len(dims))])
    return level


def shared_out(rng, own, number, rows, count, top, bound, skew):
    sequence = jax.random.permutation(rng, count)
    crowded, ordinary = shares(count, rows * top, bound, skew, True), shares(count, rows * top, bound, skew, False)
    places = jnp.arange(count)

    def named(tallies, offset_by):
        used = int((tallies > 0).sum())
        fixed = max(1, used // 4)
        passed = fixed + (places - fixed + offset_by * (used - fixed)) % max(1, count - fixed)
        return jnp.zeros((count,), jnp.int32).at[sequence[jnp.where(places < fixed, places, passed)]].set(jnp.asarray(tallies, jnp.int32))

    tallies = jnp.where(number % 4 == 0, named(crowded, number // 4), named(ordinary, number - number // 4 - 1))
    mixed = jax.random.permutation(jax.random.fold_in(own, 3), count)
    giver, taker = mixed[0:count // 2 * 2:2], mixed[1:count // 2 * 2:2]
    slack = jnp.minimum(tallies[giver] - 1, bound - tallies[taker]) // 2
    slack = jnp.where((giver == sequence[0]) | (taker == sequence[0]) | (tallies[taker] == 0), 0, jnp.maximum(slack, 0))
    passed = jax.random.randint(jax.random.fold_in(own, 4), (count // 2,), 0, 1 << 20) % (slack + 1)
    tallies = tallies.at[giver].add(-passed).at[taker].add(passed)
    labels = jnp.searchsorted(jnp.cumsum(tallies), jnp.arange(rows * top), side="right").astype(jnp.int32)
    listing = labels.reshape(top, rows).T
    listing = listing[jax.random.permutation(jax.random.fold_in(own, 1), rows)]
    offset_by = jax.random.randint(jax.random.fold_in(own, 2), (rows, 1), 0, top)
    return jnp.take_along_axis(listing, (jnp.arange(top)[None, :] + offset_by) % top, axis=1)


def shares(number_of, total, limit, lean, full):
    weights = [(1 << 20) // math.isqrt(grade ** lean) + 1 for grade in range(1, number_of + 1)]
    largest = limit if full else min(limit, max(-(-total // number_of), total * weights[0] // sum(weights)))
    least = 1 if total - largest >= number_of - 1 else 0
    holding, surplus = [largest] + [least] * (number_of - 1), total - largest - least * (number_of - 1)
    while surplus > 0:
        candidates = [i for i in range(1, number_of) if holding[i] < largest] or [i for i in range(1, number_of) if holding[i] < limit]
        pool, left = sum([weights[i] for i in candidates]), surplus
        for i in candidates:
            extra = min(limit - holding[i], max(1, left * weights[i] // pool), surplus)
            holding[i] = holding[i] + extra
            surplus = surplus - extra
    return np.array(holding)


def gaussian(rng, shape, deviation, most, pieces=(), kind=jnp.bfloat16):
    values = jax.random.normal(rng, shape, jnp.float32) * deviation
    if len(pieces) > 0:
        values = block_scale(rng, shape, pieces, -0.22, 0.18) * values
    return jnp.clip(values, min=-most, max=most).astype(kind)


def setup_inputs(seed: int = 0) -> dict:
    arg_keys = jax.random.split(jax.random.key(seed), 14)
    sky_components = gaussian(arg_keys[0], (FACETS, CORRELATION_NUM, SCALES, FS, FS), 1.0, 6.0, ((0, 8), (3, 16)))
    scale_kernels = jnp.clip(jnp.exp(jax.random.uniform(arg_keys[1], (SCALES, 2 * HALF + 1), jnp.float32, math.log(0.026111647), math.log(0.26111647))), 0.026111647, 0.26111647)
    row_taper = gaussian(arg_keys[2], (FACETS, FS, SUBROWS * CM), FS ** -0.5, 0.125, ((0, 8),))
    col_taper = gaussian(arg_keys[3], (FACETS, FS, SUBCOLS * CM), FS ** -0.5, 0.125, ((0, 8),))
    finish_rows = gaussian(arg_keys[4], (FACETS, SG, CM), (FACETS * CM) ** -0.5, 0.1875)
    finish_cols = gaussian(arg_keys[5], (FACETS, SG, CM), CM ** -0.5, 0.5)
    subgrid_owner = draw_subgrid_owner(jax.random.fold_in(arg_keys[13], 71), 0)
    block_cell = plant(jax.random.randint(arg_keys[7], (SUBGRID_COUNT * BLK, 2), 0, SG - TILE + 1), jax.random.fold_in(arg_keys[7], 1), 0, SG - TILE).astype(jnp.int32)
    vis_offset = jnp.clip(31.0 * jax.random.uniform(arg_keys[8], (SUBGRID_COUNT * BLK, 2, BLOCK_VISIBILITY), jnp.float32) ** block_scale(arg_keys[8], (SUBGRID_COUNT * BLK, 2, BLOCK_VISIBILITY), ((0, 128),), -0.2, 0.2), 0.0, 31.0)
    block_owner_keys = jax.random.split(jax.random.fold_in(arg_keys[9], 1), (SUBGRID_COUNT * BLK) // BLK)
    block_owner_turns = jax.random.permutation(jax.random.fold_in(arg_keys[9], 3), (SUBGRID_COUNT * BLK) // BLK)
    block_owner = jax.vmap(lambda own, number: shared_out(jax.random.fold_in(arg_keys[9], 2), own, number, BLK, SUBGRID_COUNT, 1, RECEIVE_BLOCKS, 2))(block_owner_keys, block_owner_turns).reshape((SUBGRID_COUNT * BLK, 1))
    observed = gaussian(arg_keys[10], (SUBGRID_COUNT * SUBGRID_COUNT * RECEIVE_BLOCKS, CORRELATION_NUM, BLOCK_VISIBILITY), 1.0, 6.0, ((0, 128),), jnp.float32)
    antenna_pair_index = plant(jax.random.randint(arg_keys[11], (SUBGRID_COUNT * SUBGRID_COUNT * RECEIVE_BLOCKS, 2, BLOCK_VISIBILITY), 0, ANTENNA_COUNT), jax.random.fold_in(arg_keys[11], 1), 0, ANTENNA_COUNT - 1).astype(jnp.int32)
    gains = jnp.clip(1.0 + 0.18 * jax.random.normal(arg_keys[12], (CORRELATION_NUM, ANTENNA_COUNT), jnp.float32), 0.1, 1.9)
    return dict(sky_components=sky_components, scale_kernels=scale_kernels, row_taper=row_taper, col_taper=col_taper, finish_rows=finish_rows, finish_cols=finish_cols, subgrid_owner=subgrid_owner, block_cell=block_cell, vis_offset=vis_offset, block_owner=block_owner, observed=observed, antenna_pair_index=antenna_pair_index, gains=gains)


KERNEL_WIDTH = 1.5


def smooth_rows_cols(padded, kernels, rows):
    taps = kernels.shape[1]
    width = (taps - 1) // 2
    along_rows = jnp.zeros(padded.shape[:2] + (rows, padded.shape[3]), jnp.float32)
    for tap in range(taps):
        along_rows = along_rows + kernels[:, tap][None, :, None, None] * padded[:, :, tap:tap + rows, :].astype(jnp.float32)
    cols = along_rows.shape[3]
    wide = jnp.pad(along_rows, ((0, 0), (0, 0), (0, 0), (width, width)))
    total = jnp.zeros_like(along_rows)
    for tap in range(taps):
        total = total + kernels[:, tap][None, :, None, None] * wide[:, :, :, tap:tap + cols]
    return jnp.sum(total, axis=1).astype(jnp.bfloat16)


def weights_of(offset):
    places = jnp.arange(TILE).astype(jnp.float32)
    delta = (places[None, None, :] - offset[:, :, None]) / KERNEL_WIDTH
    return jnp.exp(-0.5 * delta * delta)


def reference(sky_components, scale_kernels, row_taper, col_taper, finish_rows, finish_cols, subgrid_owner, block_cell, vis_offset, block_owner, observed, antenna_pair_index, gains):
    width = HALF

    def one_facet(index):
        comp = sky_components[index]
        padded = jnp.pad(comp, ((0, 0), (0, 0), (width, width), (0, 0)))
        smoothed = smooth_rows_cols(padded, scale_kernels, FS)
        col_products = jnp.einsum('crw,wk->crk', smoothed.astype(jnp.float32), col_taper[index].astype(jnp.float32)).astype(jnp.bfloat16)
        col_products = col_products.reshape(CORRELATION_NUM, FS, SUBCOLS, CM)
        rows_t = row_taper[index].reshape(FS, SUBROWS, CM)
        return jnp.einsum('rai,crbj->cabij', rows_t.astype(jnp.float32), col_products.astype(jnp.float32)).astype(jnp.bfloat16)

    contributions = lax.map(one_facet, jnp.arange(FACETS, dtype=jnp.int32))
    numbers = jnp.arange(SUBGRID_COUNT, dtype=jnp.int32)
    home = jnp.sum(jnp.where(subgrid_owner[None, :] == numbers[:, None], numbers[None, :], 0), axis=1).astype(jnp.int32)

    def one_device(device):
        grid_id = home[device]
        row_id = grid_id // SUBCOLS
        col_id = grid_id % SUBCOLS
        mine = contributions[:, :, row_id, col_id]
        spread = jnp.einsum('fcij,fsj->fcis', mine.astype(jnp.float32), finish_cols.astype(jnp.float32)).astype(jnp.bfloat16)
        subgrid = jnp.einsum('fri,fcis->crs', finish_rows.astype(jnp.float32), spread.astype(jnp.float32)).astype(jnp.bfloat16)
        cells = lax.dynamic_slice_in_dim(block_cell, device * BLK, BLK, 0)
        offsets = lax.dynamic_slice_in_dim(vis_offset, device * BLK, BLK, 0)

        def cut_tile(corner):
            return lax.dynamic_slice(subgrid, (jnp.int32(0), corner[0], corner[1]), (CORRELATION_NUM, TILE, TILE))

        tiles = jax.vmap(cut_tile)(cells)
        row_weights = weights_of(offsets[:, 0, :]).astype(jnp.bfloat16)
        col_weights = weights_of(offsets[:, 1, :])
        partial_value = jnp.einsum('kvi,kcij->kcvj', row_weights.astype(jnp.float32), tiles.astype(jnp.float32))
        predicted = jnp.sum(partial_value * col_weights[:, None, :, :], axis=3)
        return subgrid, predicted

    subgrids, predicted = lax.map(one_device, numbers)
    dest = block_owner[:, 0].reshape(SUBGRID_COUNT, BLK)
    same = dest[:, :, None] == dest[:, None, :]
    order = jnp.arange(BLK, dtype=jnp.int32)
    earlier = order[None, :] < order[:, None]
    rank = jnp.sum((same & earlier[None, :, :]).astype(jnp.int32), axis=2)
    slot = dest * (SUBGRID_COUNT * RECEIVE_BLOCKS) + numbers[:, None] * RECEIVE_BLOCKS + rank
    placed = jnp.zeros(observed.shape, jnp.float32).at[slot.reshape(-1)].set(predicted.reshape(SUBGRID_COUNT * BLK, CORRELATION_NUM, BLOCK_VISIBILITY))
    gain_p = jnp.take(gains, antenna_pair_index[:, 0, :], axis=1)
    gain_q = jnp.take(gains, antenna_pair_index[:, 1, :], axis=1)
    product = jnp.transpose(gain_p * gain_q, (1, 0, 2))
    residual = observed - product * placed
    return subgrids, residual
```

```python
import functools

import jax
import jax.numpy as jnp
from jax import lax
from jax.experimental import pallas as pl
from jax.experimental.pallas import tpu as pltpu
from jax.sharding import PartitionSpec as P

TILE = 32
KERNEL_WIDTH = 1.5
BF16 = jnp.bfloat16
F32 = jnp.float32
VMEM_LIMIT = 56 * 1024 * 1024


def dot(a, b, dims=((1,), (0,))):
    return lax.dot_general(a, b, (dims, ((), ())), preferred_element_type=F32)


def banded(kern_ref, scale, taps, first, rows):
    lane = lax.broadcasted_iota(jnp.int32, (8, 256), 1)
    base = jnp.zeros((8, 256), F32)
    for tap in range(taps):
        base = jnp.where(lane == (first[tap] % 256), kern_ref[scale, tap], base)
    wide = jnp.broadcast_to(base[:1], (rows, 256))
    return pltpu.roll(wide, 0, 1, stride=1, stride_axis=0)


def column_kernel(owner_ref, kern_ref, x_hbm, ct_hbm, out_ref, x_v, ct_v, s_v, x_sem, ct_sem, *, n_strip):
    corr, scales, rows, cols = x_hbm.shape
    taps = kern_ref.shape[1]
    half = (taps - 1) // 2
    out_rows = rows + 2 * half
    side = out_ref.shape[2] // corr
    x_parts, ct_parts = x_sem.shape[0], ct_sem.shape[0]
    x_w, ct_w = cols // x_parts, cols // ct_parts
    x_copies = [
        pltpu.make_async_copy(
            x_hbm.at[:, :, :, pl.ds(x_w * m, x_w)],
            x_v.at[:, :, :, pl.ds(128 + x_w * m, x_w)],
            x_sem.at[m],
        )
        for m in range(x_parts)
    ]
    ct_copies = [
        pltpu.make_async_copy(
            ct_hbm.at[:, pl.ds(ct_w * m, ct_w)], ct_v.at[:, pl.ds(ct_w * m, ct_w)], ct_sem.at[m]
        )
        for m in range(ct_parts)
    ]
    for copy in x_copies + ct_copies:
        copy.start()
    zeros = jnp.zeros((corr, scales, rows, 128), BF16)
    x_v[:, :, :, pl.ds(0, 128)] = zeros
    x_v[:, :, :, pl.ds(128 + cols, 128)] = zeros

    i = lax.broadcasted_iota(jnp.int32, (256, 256), 0)
    j = lax.broadcasted_iota(jnp.int32, (256, 256), 1)
    mains, edges, bands = [], [], []
    for s in range(scales):
        circ = banded(kern_ref, s, taps, [half - t for t in range(taps)], 256)
        near = jnp.abs(i - j) <= half
        mains.append(jnp.where(near, circ, 0.0).astype(BF16))
        wrap = jnp.where(near, 0.0, circ)
        edges.append(jnp.concatenate([wrap[128:], wrap[:128]], axis=0).astype(BF16))
        band = banded(kern_ref, s, taps, [t - 2 * half for t in range(taps)], out_rows)
        bands.append(band[:, :rows].astype(BF16))
    band_all = jnp.concatenate(bands, axis=1)

    for n in range(cols // 256):
        for m in range(x_parts):
            first_block = max(0, (x_w * m) // 256 - 1)
            if first_block == n:
                x_copies[m].wait()
        at = 128 + 256 * n
        ys = []
        for s in range(scales):
            mid = x_v[:, s, :, pl.ds(at, 256)].reshape(corr * rows, 256)
            before = x_v[:, s, :, pl.ds(at - 128, 128)].reshape(corr * rows, 128)
            after = x_v[:, s, :, pl.ds(at + 256, 128)].reshape(corr * rows, 128)
            side_x = jnp.concatenate([before, after], axis=1)
            ys.append((dot(mid, mains[s]) + dot(side_x, edges[s])).astype(BF16))
        for c in range(corr):
            y = jnp.concatenate([y_s[c * rows : (c + 1) * rows] for y_s in ys], axis=0)
            s_v[pl.ds(c * out_rows, out_rows), pl.ds(256 * n, 256)] = dot(band_all, y).astype(BF16)

    for m in range(ct_parts):
        ct_copies[m].wait()
        product = dot(s_v[...], ct_v[:, pl.ds(ct_w * m, ct_w)]).astype(BF16)
        for h in range(ct_w // side):
            to = lax.rem(owner_ref[m * (ct_w // side) + h], n_strip)
            for c in range(corr):
                out_ref[to, :, pl.ds(c * side, side)] = product[
                    c * out_rows : (c + 1) * out_rows, h * side : (h + 1) * side
                ]


def row_kernel(owner_ref, q_ref, rt_hbm, out_ref, rt_v, sem, *, n_strip, sub_cols):
    strips, part, _ = q_ref.shape
    rows, width = rt_hbm.shape
    each = rows // strips
    half = (part - each) // 2
    side = out_ref.shape[2]
    parts = sem.shape[0]
    w = width // parts
    copies = []
    for m in range(parts):
        for t in range(strips):
            low = max(0, t * each - half)
            high = min(rows, (t + 1) * each + half)
            to = t * part + low - (t * each - half)
            copies.append(
                pltpu.make_async_copy(
                    rt_hbm.at[pl.ds(low, high - low), pl.ds(w * m, w)],
                    rt_v.at[pl.ds(to, high - low), pl.ds(w * m, w)],
                    sem.at[m, t],
                )
            )
    for copy in copies:
        copy.start()
    rt_v[pl.ds(0, half), :] = jnp.zeros((half, width), BF16)
    rt_v[pl.ds(strips * part - half, half), :] = jnp.zeros((half, width), BF16)
    q = q_ref[...].reshape(strips * part, q_ref.shape[2])
    q_t = q.T
    for m in range(parts):
        for copy in copies[m * strips : (m + 1) * strips]:
            copy.wait()
        product = dot(q_t, rt_v[:, pl.ds(w * m, w)]).astype(BF16)
        for h in range(w // side):
            to = lax.div(owner_ref[(m * (w // side) + h) * sub_cols], n_strip)
            out_ref[to] = product[:, h * side : (h + 1) * side]


def grid_kernel(cell_ref, dest_ref, m_ref, fr_ref, fc_ref, off_ref, grid_ref, out_ref, s_v, o_v, count):
    facets, both, side = m_ref.shape
    corr = both // side
    grid = fr_ref.shape[1]
    blocks = off_ref.shape[0]
    devices = out_ref.shape[0]

    @pl.loop(0, devices)
    def _(d):
        count[d] = 0

    o_v[...] = jnp.zeros_like(o_v)
    fr = jnp.concatenate([fr_ref[f] for f in range(facets)], axis=1)
    for c in range(corr):
        spread = jnp.concatenate(
            [
                dot(fc_ref[f], m_ref[f, pl.ds(c * side, side), :]).astype(BF16)
                for f in range(facets)
            ],
            axis=1,
        )
        sub = dot(fr, spread, ((1,), (1,))).astype(BF16)
        grid_ref[c] = sub
        for h in range(grid // 128):
            s_v[c, h] = sub[:, h * 128 : (h + 1) * 128].astype(F32)

    place = lax.broadcasted_iota(jnp.int32, (TILE, 128), 0).astype(F32)
    lane = lax.broadcasted_iota(jnp.int32, (TILE, 128), 1)

    def weights(offset):
        delta = (place - offset) * (1.0 / KERNEL_WIDTH)
        return jnp.exp(-0.5 * delta * delta)

    def one(k):
        r, q = cell_ref[k, 0], cell_ref[k, 1]
        lane_tile, shift = lax.div(q, 128), lax.rem(q, 128)
        after = jnp.minimum(lane_tile + 1, grid // 128 - 1)
        tiles = []
        for c in range(corr):
            window = jnp.where(
                lane >= shift, s_v[c, lane_tile, pl.ds(r, TILE), :], s_v[c, after, pl.ds(r, TILE), :]
            )
            tiles.append(pltpu.roll(window, lax.rem(128 - shift + TILE * c, 128), 1))
        tile = tiles[0]
        for c in range(1, corr):
            tile = jnp.where(lane < TILE * c, tile, tiles[c])
        row_w = weights(off_ref[k, pl.ds(0, 1), :]).astype(BF16)
        col_w = weights(off_ref[k, pl.ds(1, 1), :])
        along = dot(tile.astype(BF16).T[: TILE * corr], row_w)
        dest = dest_ref[k, 0]
        rank = count[dest]
        count[dest] = rank + 1
        values = [
            jnp.sum(along[c * TILE : (c + 1) * TILE] * col_w, axis=0, keepdims=True) for c in range(corr)
        ]
        o_v[dest, pl.ds(rank * corr, corr), :] = jnp.concatenate(values, axis=0)

    unroll = 8 if blocks % 8 == 0 else 1

    @pl.loop(0, blocks // unroll)
    def _(g):
        for u in range(unroll):
            one(g * unroll + u)

    out_ref[...] = o_v[...].astype(BF16)


def gain_kernel(gains_ref, pair_ref, out_ref):
    corr, antennas = gains_ref.shape
    n, _, v = pair_ref.shape
    step = 8

    @pl.loop(0, n // step)
    def _(g):
        at = pl.multiple_of(g * step, step)
        product = [None] * corr
        for end in range(2):
            index = pair_ref[pl.ds(at, step), end, :]
            low = index & 127
            high = index >> 7
            for c in range(corr):
                gain = None
                for part in range(antennas // 128):
                    table = jnp.broadcast_to(gains_ref[pl.ds(c, 1), pl.ds(part * 128, 128)], (step, 128))
                    here = jnp.take_along_axis(table, low, axis=1, mode="promise_in_bounds")
                    gain = here if part == 0 else jnp.where(high == part, here, gain)
                product[c] = gain if end == 0 else product[c] * gain
        for c in range(corr):
            out_ref[pl.ds(at, step), c, :] = product[c]


VMEM = pl.BlockSpec(memory_space=pltpu.VMEM)
SMEM = pl.BlockSpec(memory_space=pltpu.SMEM)
ANY = pl.BlockSpec(memory_space=pl.ANY)


def call(kernel, name, ins, outs, shapes, scratch):
    return pl.pallas_call(
        kernel,
        in_specs=ins,
        out_specs=outs,
        out_shape=shapes,
        scratch_shapes=scratch,
        compiler_params=pltpu.CompilerParams(vmem_limit_bytes=VMEM_LIMIT),
        name=name,
    )


def on_device(
    sky_components,
    scale_kernels,
    row_taper,
    col_taper,
    finish_rows,
    finish_cols,
    subgrid_owner,
    block_cell,
    vis_offset,
    block_owner,
    observed,
    antenna_pair_index,
    gains,
):
    n_facet = lax.axis_size("facet")
    n_strip = lax.axis_size("strip")
    devices = n_facet * n_strip
    comp = sky_components[0]
    corr, scales, rows, cols = comp.shape
    facets, grid, side = finish_cols.shape
    sub_rows = row_taper.shape[2] // side
    sub_cols = col_taper.shape[2] // side
    taps = scale_kernels.shape[1]
    out_rows = rows + taps - 1
    capacity = observed.shape[0] // devices
    visibilities = observed.shape[2]

    sent = call(
        functools.partial(column_kernel, n_strip=n_strip),
        "columns",
        [SMEM, SMEM, ANY, ANY],
        VMEM,
        jax.ShapeDtypeStruct((n_strip, out_rows, corr * side), BF16),
        [
            pltpu.VMEM((corr, scales, rows, cols + 256), BF16),
            pltpu.VMEM(col_taper.shape[1:], BF16),
            pltpu.VMEM((corr * out_rows, cols), BF16),
            pltpu.SemaphoreType.DMA((4,)),
            pltpu.SemaphoreType.DMA((8,)),
        ],
    )(subgrid_owner, scale_kernels, comp, col_taper[0])
    held = lax.all_to_all(sent, "strip", split_axis=0, concat_axis=0, tiled=True)

    gain = call(
        gain_kernel,
        "gain_products",
        [VMEM, VMEM],
        VMEM,
        jax.ShapeDtypeStruct(observed.shape, F32),
        [],
    )(gains, antenna_pair_index)

    parted = call(
        functools.partial(row_kernel, n_strip=n_strip, sub_cols=sub_cols),
        "rows",
        [SMEM, VMEM, ANY],
        VMEM,
        jax.ShapeDtypeStruct((n_facet, corr * side, side), BF16),
        [
            pltpu.VMEM((n_strip * out_rows, row_taper.shape[2]), BF16),
            pltpu.SemaphoreType.DMA((4, n_strip)),
        ],
    )(subgrid_owner, held, row_taper[0])
    mine = lax.all_to_all(parted, "facet", split_axis=0, concat_axis=0, tiled=True)

    subgrid, outgoing = call(
        grid_kernel,
        "subgrid_and_degrid",
        [SMEM, SMEM, VMEM, VMEM, VMEM, VMEM],
        [VMEM, VMEM],
        [
            jax.ShapeDtypeStruct((corr, grid, grid), BF16),
            jax.ShapeDtypeStruct((devices, capacity * corr, visibilities), BF16),
        ],
        [
            pltpu.VMEM((corr, grid // 128, grid, 128), F32),
            pltpu.VMEM((devices, capacity * corr, visibilities), F32),
            pltpu.SMEM((devices,), jnp.int32),
        ],
    )(block_cell, block_owner, mine, finish_rows, finish_cols, vis_offset)
    arrived = lax.all_to_all(outgoing, ("facet", "strip"), split_axis=0, concat_axis=0, tiled=True)
    placed = arrived.astype(F32).reshape(devices * capacity, corr, visibilities)
    return (subgrid[None], observed - gain * placed)


def solution(mesh):
    placed = (
        P("facet", None, None, "strip", None),
        P(),
        P("facet", None, None),
        P("facet", None, None),
        P(),
        P(),
        P(),
        P(("facet", "strip"), None),
        P(("facet", "strip"), None, None),
        P(("facet", "strip"), None),
        P(("facet", "strip"), None, None),
        P(("facet", "strip"), None, None),
        P(),
    )
    return jax.shard_map(
        on_device,
        mesh=mesh,
        in_specs=placed,
        out_specs=(P(("facet", "strip"), None, None, None), P(("facet", "strip"), None, None)),
        check_vma=False,
    )
```

```python
import functools

import jax
import jax.numpy as jnp
from jax import lax
from jax.experimental import pallas as pl
from jax.experimental.pallas import tpu as pltpu
from jax.sharding import PartitionSpec as P

TILE = 32
KERNEL_WIDTH = 1.5
BF16 = jnp.bfloat16
F32 = jnp.float32


def dot(a, b, dims=((1,), (0,))):
    return lax.dot_general(a, b, (dims, ((), ())), preferred_element_type=F32)


def stacked(rows):
    return jnp.concatenate([jnp.concatenate(row, axis=1) for row in rows], axis=0)


def circulant(kern_ref, scale, places, rows):
    lane = lax.broadcasted_iota(jnp.int32, (8, 256), 1)
    base = jnp.zeros((8, 256), F32)
    for tap, place in enumerate(places):
        base = jnp.where(lane == place % 256, kern_ref[scale, tap], base)
    return pltpu.roll(jnp.broadcast_to(base[:1], (rows, 256)), 0, 1, stride=1, stride_axis=0)


def column_kernel(owner_ref, kern_ref, x_hbm, ct_hbm, out_ref, x_v, ct_v, s_v, x_sem, ct_sem, *, n_strip):
    corr, scales, rows, cols = x_hbm.shape
    taps = kern_ref.shape[1]
    half = (taps - 1) // 2
    out_rows = rows + 2 * half
    side = out_ref.shape[2] // corr
    x_parts, ct_parts = x_sem.shape[0], ct_sem.shape[0]
    x_w, ct_w = cols // x_parts, cols // ct_parts
    x_copies = [
        pltpu.make_async_copy(
            x_hbm.at[:, :, :, pl.ds(x_w * m, x_w)],
            x_v.at[:, :, :, pl.ds(128 + x_w * m, x_w)],
            x_sem.at[m],
        )
        for m in range(x_parts)
    ]
    ct_copies = [
        pltpu.make_async_copy(
            ct_hbm.at[:, pl.ds(ct_w * m, ct_w)], ct_v.at[:, pl.ds(ct_w * m, ct_w)], ct_sem.at[m]
        )
        for m in range(ct_parts)
    ]
    for copy in x_copies + ct_copies:
        copy.start()
    zeros = jnp.zeros((corr, scales, rows, 128), BF16)
    x_v[:, :, :, pl.ds(0, 128)] = zeros
    x_v[:, :, :, pl.ds(128 + cols, 128)] = zeros

    mains, edges, bands = [], [], []
    blank = jnp.zeros((64, 128), F32)
    zero = jnp.zeros((128, 128), BF16)
    for s in range(scales):
        wide = circulant(kern_ref, s, [half - t for t in range(taps)], 128)
        same, wrap = wide[:, :128].astype(BF16), wide[:, 128:]
        before = jnp.concatenate([blank, wrap[64:]], axis=0).astype(BF16)
        after = jnp.concatenate([wrap[:64], blank], axis=0).astype(BF16)
        mains.append(stacked([[same, before], [after, same]]))
        edges.append(stacked([[before, zero], [zero, after]]))
        bands.append(circulant(kern_ref, s, [t - 2 * half for t in range(taps)], out_rows)[:, :rows].astype(BF16))
    band_all = jnp.concatenate(bands, axis=1)

    for n in range(cols // 256):
        for m in range(x_parts):
            first_block = max(0, (x_w * m) // 256 - 1)
            if first_block == n:
                x_copies[m].wait()
        at = 128 + 256 * n
        ys = []
        for s in range(scales):
            mid = x_v[:, s, :, pl.ds(at, 256)].reshape(corr * rows, 256)
            before = x_v[:, s, :, pl.ds(at - 128, 128)].reshape(corr * rows, 128)
            after = x_v[:, s, :, pl.ds(at + 256, 128)].reshape(corr * rows, 128)
            side_x = jnp.concatenate([before, after], axis=1)
            ys.append((dot(mid, mains[s]) + dot(side_x, edges[s])).astype(BF16))
        for c in range(corr):
            y = jnp.concatenate([y_s[c * rows : (c + 1) * rows] for y_s in ys], axis=0)
            s_v[pl.ds(c * out_rows, out_rows), pl.ds(256 * n, 256)] = dot(band_all, y).astype(BF16)

    for m in range(ct_parts):
        ct_copies[m].wait()
        product = dot(s_v[...], ct_v[:, pl.ds(ct_w * m, ct_w)]).astype(BF16)
        for h in range(ct_w // side):
            to = lax.rem(owner_ref[m * (ct_w // side) + h], n_strip)
            for c in range(corr):
                out_ref[to, :, pl.ds(c * side, side)] = product[
                    c * out_rows : (c + 1) * out_rows, h * side : (h + 1) * side
                ]


def row_kernel(owner_ref, q_ref, rt_ref, out_ref, *, n_strip, sub_cols):
    strips, part, _ = q_ref.shape
    each = rt_ref.shape[0] // strips
    half = (part - each) // 2
    side = out_ref.shape[2]
    rows = []
    for t in range(strips):
        head = q_ref[t, pl.ds(half, half), :]
        tail = q_ref[t, pl.ds(each, half), :]
        if t > 0:
            head = (head.astype(F32) + q_ref[t - 1, pl.ds(half + each, half), :].astype(F32)).astype(BF16)
        if t < strips - 1:
            tail = (tail.astype(F32) + q_ref[t + 1, pl.ds(0, half), :].astype(F32)).astype(BF16)
        rows += [head, q_ref[t, pl.ds(2 * half, each - 2 * half), :], tail]
    product = dot(jnp.concatenate(rows, axis=0).T, rt_ref[...]).astype(BF16)
    for a in range(out_ref.shape[0]):
        to = lax.div(owner_ref[a * sub_cols], n_strip)
        for c in range(out_ref.shape[1] // side):
            out_ref[to, pl.ds(c * side, side), :] = product[
                c * side : (c + 1) * side, a * side : (a + 1) * side
            ].T


def grid_kernel(cell_ref, dest_ref, m_ref, fr_ref, fc_ref, off_ref, grid_ref, out_ref, s_v, o_v, count):
    facets, both, side = m_ref.shape
    corr = both // side
    grid = fr_ref.shape[1]
    blocks = off_ref.shape[0]
    devices = out_ref.shape[0]

    @pl.loop(0, devices)
    def _(d):
        count[d] = 0

    o_v[...] = jnp.zeros_like(o_v)
    fr = jnp.concatenate([fr_ref[f] for f in range(facets)], axis=1)
    spreads = [dot(m_ref[f], fc_ref[f], ((1,), (1,))).astype(BF16) for f in range(facets)]
    for c in range(corr):
        spread = jnp.concatenate([one_f[c * side : (c + 1) * side] for one_f in spreads], axis=0)
        sub = dot(fr, spread).astype(BF16)
        grid_ref[c] = sub
        for h in range(grid // 128):
            s_v[c, h] = sub[:, h * 128 : (h + 1) * 128].astype(F32)

    lane = lax.broadcasted_iota(jnp.int32, (TILE, 128), 1)
    place = lax.broadcasted_iota(jnp.int32, (TILE, 128), 0).astype(F32)

    def weights(offset):
        delta = (place - offset) * (1.0 / KERNEL_WIDTH)
        return jnp.exp(-0.5 * delta * delta)

    def one(k):
        r, q = cell_ref[k, 0], cell_ref[k, 1]
        lane_tile, shift = lax.div(q, 128), lax.rem(q, 128)
        after = jnp.minimum(lane_tile + 1, grid // 128 - 1)
        tiles = []
        for c in range(corr):
            window = jnp.where(
                lane >= shift, s_v[c, lane_tile, pl.ds(r, TILE), :], s_v[c, after, pl.ds(r, TILE), :]
            )
            tiles.append(pltpu.roll(window, lax.rem(128 - shift + TILE * c, 128), 1))
        tile = tiles[0]
        for c in range(1, corr):
            tile = jnp.where(lane < TILE * c, tile, tiles[c])
        row_w = weights(off_ref[k, pl.ds(0, 1), :]).astype(BF16)
        col_w = weights(off_ref[k, pl.ds(1, 1), :])
        along = dot(tile.astype(BF16).T[: TILE * corr], row_w)
        dest = dest_ref[k, 0]
        rank = count[dest]
        count[dest] = rank + 1
        values = [
            jnp.sum(along[c * TILE : (c + 1) * TILE] * col_w, axis=0, keepdims=True) for c in range(corr)
        ]
        o_v[dest, pl.ds(rank * corr, corr), :] = jnp.concatenate(values, axis=0)

    unroll = 8 if blocks % 8 == 0 else 1

    @pl.loop(0, blocks // unroll)
    def _(g):
        for u in range(unroll):
            one(g * unroll + u)

    out_ref[...] = o_v[...].astype(BF16)


def gain_kernel(gains_ref, pair_ref, out_ref):
    corr, antennas = gains_ref.shape
    n, _, v = pair_ref.shape
    step = 32

    @pl.loop(0, n // step)
    def _(g):
        at = pl.multiple_of(g * step, step)
        product = [None] * corr
        for end in range(2):
            index = pair_ref[pl.ds(at, step), end, :]
            low = index & 127
            high = index >> 7
            for c in range(corr):
                gain = None
                for part in range(antennas // 128):
                    table = jnp.broadcast_to(gains_ref[pl.ds(c, 1), pl.ds(part * 128, 128)], (step, 128))
                    here = jnp.take_along_axis(table, low, axis=1, mode="promise_in_bounds")
                    gain = here if part == 0 else jnp.where(high == part, here, gain)
                product[c] = gain if end == 0 else product[c] * gain
        for c in range(corr):
            out_ref[pl.ds(at, step), c, :] = product[c]


VMEM = pl.BlockSpec(memory_space=pltpu.VMEM)
SMEM = pl.BlockSpec(memory_space=pltpu.SMEM)
HBM = pl.BlockSpec(memory_space=pltpu.HBM)


def residual_kernel(observed_ref, gain_ref, placed_ref, out_ref):
    out_ref[...] = observed_ref[...] - gain_ref[...] * placed_ref[...].astype(F32)


def call(kernel, name, ins, outs, shapes, scratch, mib):
    return pl.pallas_call(
        kernel,
        in_specs=ins,
        out_specs=outs,
        out_shape=shapes,
        scratch_shapes=scratch,
        compiler_params=pltpu.CompilerParams(vmem_limit_bytes=mib * 1024 * 1024),
        name=name,
    )


def in_vmem(x):
    return pltpu.with_memory_space_constraint(x, pltpu.VMEM)


def in_hbm(x):
    return pltpu.with_memory_space_constraint(x, pltpu.HBM)


def on_device(
    sky_components,
    scale_kernels,
    row_taper,
    col_taper,
    finish_rows,
    finish_cols,
    subgrid_owner,
    block_cell,
    vis_offset,
    block_owner,
    observed,
    antenna_pair_index,
    gains,
):
    n_facet = lax.axis_size("facet")
    n_strip = lax.axis_size("strip")
    devices = n_facet * n_strip
    comp = sky_components[0]
    corr, scales, rows, cols = comp.shape
    facets, grid, side = finish_cols.shape
    sub_rows = row_taper.shape[2] // side
    sub_cols = col_taper.shape[2] // side
    taps = scale_kernels.shape[1]
    out_rows = rows + taps - 1
    capacity = observed.shape[0] // devices
    visibilities = observed.shape[2]

    sent = call(
        functools.partial(column_kernel, n_strip=n_strip),
        "columns",
        [SMEM, SMEM, HBM, HBM],
        VMEM,
        pltpu.VMEM((n_strip, out_rows, corr * side), BF16),
        [
            pltpu.VMEM((corr, scales, rows, cols + 256), BF16),
            pltpu.VMEM(col_taper.shape[1:], BF16),
            pltpu.VMEM((corr * out_rows, cols), BF16),
            pltpu.SemaphoreType.DMA((4,)),
            pltpu.SemaphoreType.DMA((1,)),
        ],
        28,
    )(in_hbm(subgrid_owner), in_hbm(scale_kernels), in_hbm(comp), in_hbm(col_taper[0]))
    held = lax.all_to_all(sent, "strip", split_axis=0, concat_axis=0, tiled=True)

    parted = call(
        functools.partial(row_kernel, n_strip=n_strip, sub_cols=sub_cols),
        "rows",
        [SMEM, VMEM, VMEM],
        VMEM,
        pltpu.HBM((n_facet, corr * side, side), BF16),
        [],
        20,
    )(subgrid_owner, in_vmem(held), in_vmem(row_taper[0]))
    mine = lax.all_to_all(parted, "facet", split_axis=0, concat_axis=0, tiled=True)

    gain = call(
        gain_kernel,
        "gain_products",
        [VMEM, VMEM],
        VMEM,
        pltpu.VMEM(observed.shape, F32),
        [],
        8,
    )(gains, antenna_pair_index)

    subgrid, outgoing = call(
        grid_kernel,
        "subgrid_and_degrid",
        [SMEM, SMEM, VMEM, VMEM, VMEM, VMEM],
        [VMEM, VMEM],
        [
            jax.ShapeDtypeStruct((corr, grid, grid), BF16),
            pltpu.HBM((devices, capacity * corr, visibilities), BF16),
        ],
        [
            pltpu.VMEM((corr, grid // 128, grid, 128), F32),
            pltpu.VMEM((devices, capacity * corr, visibilities), F32),
            pltpu.SMEM((devices,), jnp.int32),
        ],
        20,
    )(
        block_cell,
        block_owner,
        in_vmem(mine),
        in_vmem(finish_rows),
        in_vmem(finish_cols),
        in_vmem(vis_offset),
    )
    arrived = lax.all_to_all(outgoing, ("facet", "strip"), split_axis=0, concat_axis=0, tiled=True)
    merged = (devices, capacity * corr, visibilities)
    residual = call(
        residual_kernel, "residual", [VMEM, VMEM, VMEM], VMEM, jax.ShapeDtypeStruct(merged, F32), [], 8
    )(in_vmem(observed.reshape(merged)), in_vmem(gain.reshape(merged)), in_vmem(arrived))
    return (subgrid[None], residual.reshape(observed.shape))


def solution(mesh):
    placed = (
        P("facet", None, None, "strip", None),
        P(),
        P("facet", None, None),
        P("facet", None, None),
        P(),
        P(),
        P(),
        P(("facet", "strip"), None),
        P(("facet", "strip"), None, None),
        P(("facet", "strip"), None),
        P(("facet", "strip"), None, None),
        P(("facet", "strip"), None, None),
        P(),
    )
    return jax.shard_map(
        on_device,
        mesh=mesh,
        in_specs=placed,
        out_specs=(P(("facet", "strip"), None, None, None), P(("facet", "strip"), None, None)),
        check_vma=False,
    )
```

```python
import functools

import jax
import jax.numpy as jnp
from jax import lax
from jax.experimental import pallas as pl
from jax.experimental.pallas import tpu as pltpu
from jax.sharding import PartitionSpec as P

TILE = 32
KERNEL_WIDTH = 1.5
BF16 = jnp.bfloat16
F32 = jnp.float32


def dot(a, b, dims=((1,), (0,))):
    return lax.dot_general(a, b, (dims, ((), ())), preferred_element_type=F32)


def stacked(rows):
    return jnp.concatenate([jnp.concatenate(row, axis=1) for row in rows], axis=0)


def circulant(kern_ref, scale, places, rows):
    lane = lax.broadcasted_iota(jnp.int32, (8, 256), 1)
    base = jnp.zeros((8, 256), F32)
    for tap, place in enumerate(places):
        base = jnp.where(lane == place % 256, kern_ref[scale, tap], base)
    return pltpu.roll(jnp.broadcast_to(base[:1], (rows, 256)), 0, 1, stride=1, stride_axis=0)


def column_kernel(owner_ref, kern_ref, x_hbm, ct_hbm, out_ref, x_v, ct_v, y_v, s_v, x_sem, ct_sem, *, n_strip):
    corr, scales, rows, cols = x_hbm.shape
    taps = kern_ref.shape[1]
    half = (taps - 1) // 2
    out_rows = rows + 2 * half
    side = out_ref.shape[2] // corr
    x_parts, ct_parts = x_sem.shape[0], ct_sem.shape[0]
    x_w, ct_w = cols // x_parts, cols // ct_parts
    x_copies = [
        pltpu.make_async_copy(
            x_hbm.at[:, :, :, pl.ds(x_w * m, x_w)],
            x_v.at[:, :, :, pl.ds(128 + x_w * m, x_w)],
            x_sem.at[m],
        )
        for m in range(x_parts)
    ]
    ct_copies = [
        pltpu.make_async_copy(
            ct_hbm.at[:, pl.ds(ct_w * m, ct_w)], ct_v.at[:, pl.ds(ct_w * m, ct_w)], ct_sem.at[m]
        )
        for m in range(ct_parts)
    ]
    for copy in x_copies:
        copy.start()
    zeros = jnp.zeros((corr, scales, rows, 128), BF16)
    x_v[:, :, :, pl.ds(0, 128)] = zeros
    x_v[:, :, :, pl.ds(128 + cols, 128)] = zeros

    columns, bands = [], []
    blank = jnp.zeros((64, 128), F32)
    zero = jnp.zeros((128, 128), BF16)
    for s in range(scales):
        wide = circulant(kern_ref, s, [half - t for t in range(taps)], 128)
        same, wrap = wide[:, :128].astype(BF16), wide[:, 128:]
        before = jnp.concatenate([blank, wrap[64:]], axis=0).astype(BF16)
        after = jnp.concatenate([wrap[:64], blank], axis=0).astype(BF16)
        columns.append(stacked([[same, before], [after, same], [before, zero], [zero, after]]))
        bands.append(circulant(kern_ref, s, [t - 2 * half for t in range(taps)], out_rows)[:, :rows].astype(BF16))
    band_all = jnp.concatenate(bands, axis=1)

    for n in range(cols // 256):
        for m in range(x_parts):
            if max(0, (x_w * m) // 256 - 1) == n:
                x_copies[m].wait()
                if m == min(1, x_parts - 1):
                    for copy in ct_copies:
                        copy.start()
        at = 128 + 256 * n
        for s in range(scales):
            mid = x_v[:, s, :, pl.ds(at, 256)].reshape(corr * rows, 256)
            before = x_v[:, s, :, pl.ds(at - 128, 128)].reshape(corr * rows, 128)
            after = x_v[:, s, :, pl.ds(at + 256, 128)].reshape(corr * rows, 128)
            y = dot(jnp.concatenate([mid, before, after], axis=1), columns[s]).astype(BF16)
            for c in range(corr):
                y_v[c, pl.ds(s * rows, rows), pl.ds(256 * n, 256)] = y[c * rows : (c + 1) * rows]
        if n % 2 == 1:
            pair = pl.ds(256 * (n - 1), 512)
            for c in range(corr):
                s_v[pl.ds(c * out_rows, out_rows), pair] = dot(band_all, y_v[c, :, pair]).astype(BF16)

    for m in range(ct_parts):
        ct_copies[m].wait()
        product = dot(s_v[...], ct_v[:, pl.ds(ct_w * m, ct_w)]).astype(BF16)
        for h in range(ct_w // side):
            to = lax.rem(owner_ref[m * (ct_w // side) + h], n_strip)
            for c in range(corr):
                out_ref[to, :, pl.ds(c * side, side)] = product[
                    c * out_rows : (c + 1) * out_rows, h * side : (h + 1) * side
                ]


def row_kernel(owner_ref, q_ref, rt_ref, out_ref, *, n_strip, sub_cols):
    strips, part, _ = q_ref.shape
    each = rt_ref.shape[0] // strips
    half = (part - each) // 2
    side = out_ref.shape[2]
    rows = []
    for t in range(strips):
        head = q_ref[t, pl.ds(half, half), :]
        tail = q_ref[t, pl.ds(each, half), :]
        if t > 0:
            head = (head.astype(F32) + q_ref[t - 1, pl.ds(half + each, half), :].astype(F32)).astype(BF16)
        if t < strips - 1:
            tail = (tail.astype(F32) + q_ref[t + 1, pl.ds(0, half), :].astype(F32)).astype(BF16)
        rows += [head, q_ref[t, pl.ds(2 * half, each - 2 * half), :], tail]
    product = dot(jnp.concatenate(rows, axis=0).T, rt_ref[...]).astype(BF16)
    for a in range(out_ref.shape[0]):
        to = lax.div(owner_ref[a * sub_cols], n_strip)
        for c in range(out_ref.shape[1] // side):
            out_ref[to, pl.ds(c * side, side), :] = product[
                c * side : (c + 1) * side, a * side : (a + 1) * side
            ].T


def grid_kernel(cell_ref, dest_ref, m_ref, fr_ref, fc_ref, off_ref, grid_hbm, out_ref, g_v, s_v, o_v, count, sem):
    facets, both, side = m_ref.shape
    corr = both // side
    grid = fr_ref.shape[1]
    blocks = off_ref.shape[0]
    devices = out_ref.shape[0]

    for d in range(devices):
        count[d] = 0
    o_v[...] = jnp.zeros_like(o_v)
    copies = [pltpu.make_async_copy(g_v.at[c], grid_hbm.at[c], sem.at[c]) for c in range(corr)]
    fr = jnp.concatenate([fr_ref[f] for f in range(facets)], axis=1)
    spreads = [dot(m_ref[f], fc_ref[f], ((1,), (1,))).astype(BF16) for f in range(facets)]
    for c in range(corr):
        spread = jnp.concatenate([one_f[c * side : (c + 1) * side] for one_f in spreads], axis=0)
        sub = dot(fr, spread).astype(BF16)
        g_v[c] = sub
        copies[c].start()
        for h in range(grid // 128):
            s_v[c, h] = sub[:, h * 128 : (h + 1) * 128].astype(F32)

    lane = lax.broadcasted_iota(jnp.int32, (TILE, 128), 1)
    place = lax.broadcasted_iota(jnp.int32, (TILE, 128), 0).astype(F32)

    def weights(offset):
        delta = (place - offset) * (1.0 / KERNEL_WIDTH)
        return jnp.exp(-0.5 * delta * delta)

    def one(k):
        r, q = cell_ref[0, k], cell_ref[1, k]
        lane_tile, shift = lax.div(q, 128), lax.rem(q, 128)
        after = jnp.minimum(lane_tile + 1, grid // 128 - 1)
        tiles = []
        for c in range(corr):
            window = jnp.where(
                lane >= shift, s_v[c, lane_tile, pl.ds(r, TILE), :], s_v[c, after, pl.ds(r, TILE), :]
            )
            tiles.append(pltpu.roll(window, lax.rem(128 - shift + TILE * c, 128), 1))
        tile = tiles[0]
        for c in range(1, corr):
            tile = jnp.where(lane < TILE * c, tile, tiles[c])
        row_w = weights(off_ref[k, pl.ds(0, 1), :]).astype(BF16)
        col_w = weights(off_ref[k, pl.ds(1, 1), :])
        along = dot(tile.astype(BF16).T[: TILE * corr], row_w)
        dest = dest_ref[0, k]
        rank = count[dest]
        count[dest] = rank + 1
        values = [
            jnp.sum(along[c * TILE : (c + 1) * TILE] * col_w, axis=0, keepdims=True) for c in range(corr)
        ]
        o_v[dest, pl.ds(rank * corr, corr), :] = jnp.concatenate(values, axis=0)

    unroll = 32 if blocks % 32 == 0 else 1

    @pl.loop(0, blocks // unroll)
    def _(g):
        for u in range(unroll):
            one(g * unroll + u)

    out_ref[...] = o_v[...].astype(BF16)
    for copy in copies:
        copy.wait()


def gain_kernel(gains_ref, pair_ref, out_ref):
    corr, antennas = gains_ref.shape
    n, _, v = pair_ref.shape
    step = 32

    @pl.loop(0, n // step)
    def _(g):
        at = pl.multiple_of(g * step, step)
        product = [None] * corr
        for end in range(2):
            index = pair_ref[pl.ds(at, step), end, :]
            low = index & 127
            high = index >> 7
            for c in range(corr):
                gain = None
                for part in range(antennas // 128):
                    table = jnp.broadcast_to(gains_ref[pl.ds(c, 1), pl.ds(part * 128, 128)], (step, 128))
                    here = jnp.take_along_axis(table, low, axis=1, mode="promise_in_bounds")
                    gain = here if part == 0 else jnp.where(high == part, here, gain)
                product[c] = gain if end == 0 else product[c] * gain
        for c in range(corr):
            out_ref[pl.ds(at, step), c, :] = product[c]


VMEM = pl.BlockSpec(memory_space=pltpu.VMEM)
SMEM = pl.BlockSpec(memory_space=pltpu.SMEM)
HBM = pl.BlockSpec(memory_space=pltpu.HBM)


def residual_kernel(observed_ref, gain_ref, placed_ref, out_ref):
    out_ref[...] = observed_ref[...] - gain_ref[...] * placed_ref[...].astype(F32)


def call(kernel, name, ins, outs, shapes, scratch, mib):
    return pl.pallas_call(
        kernel,
        in_specs=ins,
        out_specs=outs,
        out_shape=shapes,
        scratch_shapes=scratch,
        compiler_params=pltpu.CompilerParams(vmem_limit_bytes=mib * 1024 * 1024),
        name=name,
    )


def in_vmem(x):
    return pltpu.with_memory_space_constraint(x, pltpu.VMEM)


def in_hbm(x):
    return pltpu.with_memory_space_constraint(x, pltpu.HBM)


def on_device(
    sky_components,
    scale_kernels,
    row_taper,
    col_taper,
    finish_rows,
    finish_cols,
    subgrid_owner,
    block_cell,
    vis_offset,
    block_owner,
    observed,
    antenna_pair_index,
    gains,
):
    n_facet = lax.axis_size("facet")
    n_strip = lax.axis_size("strip")
    devices = n_facet * n_strip
    comp = sky_components[0]
    corr, scales, rows, cols = comp.shape
    facets, grid, side = finish_cols.shape
    sub_rows = row_taper.shape[2] // side
    sub_cols = col_taper.shape[2] // side
    taps = scale_kernels.shape[1]
    out_rows = rows + taps - 1
    capacity = observed.shape[0] // devices
    visibilities = observed.shape[2]

    sent = call(
        functools.partial(column_kernel, n_strip=n_strip),
        "columns",
        [SMEM, SMEM, HBM, HBM],
        VMEM,
        pltpu.VMEM((n_strip, out_rows, corr * side), BF16),
        [
            pltpu.VMEM((corr, scales, rows, cols + 256), BF16),
            pltpu.VMEM(col_taper.shape[1:], BF16),
            pltpu.VMEM((corr, scales * rows, cols), BF16),
            pltpu.VMEM((corr * out_rows, cols), BF16),
            pltpu.SemaphoreType.DMA((4,)),
            pltpu.SemaphoreType.DMA((2,)),
        ],
        32,
    )(in_hbm(subgrid_owner), in_hbm(scale_kernels), in_hbm(comp), in_hbm(col_taper[0]))
    held = lax.all_to_all(sent, "strip", split_axis=0, concat_axis=0, tiled=True)

    parted = call(
        functools.partial(row_kernel, n_strip=n_strip, sub_cols=sub_cols),
        "rows",
        [SMEM, VMEM, VMEM],
        VMEM,
        pltpu.HBM((n_facet, corr * side, side), BF16),
        [],
        20,
    )(subgrid_owner, in_vmem(held), in_vmem(row_taper[0]))
    mine = lax.all_to_all(parted, "facet", split_axis=0, concat_axis=0, tiled=True)

    gain = call(
        gain_kernel,
        "gain_products",
        [VMEM, VMEM],
        VMEM,
        pltpu.VMEM(observed.shape, F32),
        [],
        8,
    )(gains, antenna_pair_index)

    subgrid, outgoing = call(
        grid_kernel,
        "subgrid_and_degrid",
        [SMEM, SMEM, VMEM, VMEM, VMEM, VMEM],
        [HBM, VMEM],
        [
            jax.ShapeDtypeStruct((corr, grid, grid), BF16),
            pltpu.HBM((devices, capacity * corr, visibilities), BF16),
        ],
        [
            pltpu.VMEM((corr, grid, grid), BF16),
            pltpu.VMEM((corr, grid // 128, grid, 128), F32),
            pltpu.VMEM((devices, capacity * corr, visibilities), F32),
            pltpu.SMEM((devices,), jnp.int32),
            pltpu.SemaphoreType.DMA((corr,)),
        ],
        20,
    )(
        block_cell.T,
        block_owner.T,
        in_vmem(mine),
        in_vmem(finish_rows),
        in_vmem(finish_cols),
        in_vmem(vis_offset),
    )
    arrived = lax.all_to_all(outgoing, ("facet", "strip"), split_axis=0, concat_axis=0, tiled=True)
    merged = (devices, capacity * corr, visibilities)
    residual = call(
        residual_kernel, "residual", [VMEM, VMEM, VMEM], VMEM, jax.ShapeDtypeStruct(merged, F32), [], 8
    )(in_vmem(observed.reshape(merged)), in_vmem(gain.reshape(merged)), in_vmem(arrived))
    return (subgrid[None], residual.reshape(observed.shape))


def solution(mesh):
    placed = (
        P("facet", None, None, "strip", None),
        P(),
        P("facet", None, None),
        P("facet", None, None),
        P(),
        P(),
        P(),
        P(("facet", "strip"), None),
        P(("facet", "strip"), None, None),
        P(("facet", "strip"), None),
        P(("facet", "strip"), None, None),
        P(("facet", "strip"), None, None),
        P(),
    )
    return jax.shard_map(
        on_device,
        mesh=mesh,
        in_specs=placed,
        out_specs=(P(("facet", "strip"), None, None, None), P(("facet", "strip"), None, None)),
        check_vma=False,
    )
```

```python
import functools

import jax
import jax.numpy as jnp
from jax import lax
from jax.experimental import pallas as pl
from jax.experimental.pallas import tpu as pltpu
from jax.sharding import PartitionSpec as P

TILE = 32
KERNEL_WIDTH = 1.5
BF16 = jnp.bfloat16
F32 = jnp.float32


def dot(a, b, dims=((1,), (0,))):
    return lax.dot_general(a, b, (dims, ((), ())), preferred_element_type=F32)


def stacked(rows):
    return jnp.concatenate([jnp.concatenate(row, axis=1) for row in rows], axis=0)


def circulant(kern_ref, scale, places, rows):
    lane = lax.broadcasted_iota(jnp.int32, (8, 256), 1)
    base = jnp.zeros((8, 256), F32)
    for tap, place in enumerate(places):
        base = jnp.where(lane == place % 256, kern_ref[scale, tap], base)
    return pltpu.roll(jnp.broadcast_to(base[:1], (rows, 256)), 0, 1, stride=1, stride_axis=0)


def column_kernel(owner_ref, kern_ref, x_hbm, ct_hbm, out_ref, x_v, ct_v, y_v, s_v, x_sem, ct_sem, *, n_strip):
    corr, scales, rows, cols = x_hbm.shape
    taps = kern_ref.shape[1]
    half = (taps - 1) // 2
    out_rows = rows + 2 * half
    side = out_ref.shape[2] // corr
    x_parts, ct_parts = x_sem.shape[0], ct_sem.shape[0]
    x_w, ct_w = cols // x_parts, cols // ct_parts
    x_copies = [
        pltpu.make_async_copy(
            x_hbm.at[:, :, :, pl.ds(x_w * m, x_w)],
            x_v.at[:, :, :, pl.ds(128 + x_w * m, x_w)],
            x_sem.at[m],
        )
        for m in range(x_parts)
    ]
    ct_copies = [
        pltpu.make_async_copy(
            ct_hbm.at[:, pl.ds(ct_w * m, ct_w)], ct_v.at[:, pl.ds(ct_w * m, ct_w)], ct_sem.at[m]
        )
        for m in range(ct_parts)
    ]
    for copy in x_copies:
        copy.start()
    zeros = jnp.zeros((corr, scales, rows, 128), BF16)
    x_v[:, :, :, pl.ds(0, 128)] = zeros
    x_v[:, :, :, pl.ds(128 + cols, 128)] = zeros

    columns, bands = [], []
    blank = jnp.zeros((64, 128), F32)
    zero = jnp.zeros((128, 128), BF16)
    for s in range(scales):
        wide = circulant(kern_ref, s, [half - t for t in range(taps)], 128)
        same, wrap = wide[:, :128].astype(BF16), wide[:, 128:]
        before = jnp.concatenate([blank, wrap[64:]], axis=0).astype(BF16)
        after = jnp.concatenate([wrap[:64], blank], axis=0).astype(BF16)
        columns.append(stacked([[same, before], [after, same], [before, zero], [zero, after]]))
        bands.append(circulant(kern_ref, s, [t - 2 * half for t in range(taps)], out_rows)[:, :rows].astype(BF16))
    band_all = jnp.concatenate(bands, axis=1)

    for n in range(cols // 256):
        for m in range(x_parts):
            if max(0, (x_w * m) // 256 - 1) == n:
                x_copies[m].wait()
                if m == min(1, x_parts - 1):
                    for copy in ct_copies:
                        copy.start()
        at = 128 + 256 * n
        for s in range(scales):
            mid = x_v[:, s, :, pl.ds(at, 256)].reshape(corr * rows, 256)
            before = x_v[:, s, :, pl.ds(at - 128, 128)].reshape(corr * rows, 128)
            after = x_v[:, s, :, pl.ds(at + 256, 128)].reshape(corr * rows, 128)
            y = dot(jnp.concatenate([mid, before, after], axis=1), columns[s]).astype(BF16)
            for c in range(corr):
                y_v[c, pl.ds(s * rows, rows), pl.ds(256 * n, 256)] = y[c * rows : (c + 1) * rows]
        if n % 2 == 1:
            pair = pl.ds(256 * (n - 1), 512)
            for c in range(corr):
                s_v[pl.ds(c * out_rows, out_rows), pair] = dot(band_all, y_v[c, :, pair]).astype(BF16)

    for m in range(ct_parts):
        ct_copies[m].wait()
        product = dot(s_v[...], ct_v[:, pl.ds(ct_w * m, ct_w)]).astype(BF16)
        for h in range(ct_w // side):
            to = lax.rem(owner_ref[m * (ct_w // side) + h], n_strip)
            for c in range(corr):
                out_ref[to, :, pl.ds(c * side, side)] = product[
                    c * out_rows : (c + 1) * out_rows, h * side : (h + 1) * side
                ]


def row_kernel(owner_ref, q_ref, rt_ref, out_ref, *, n_strip, sub_cols):
    strips, part, _ = q_ref.shape
    each = rt_ref.shape[0] // strips
    half = (part - each) // 2
    side = out_ref.shape[2]
    rows = []
    for t in range(strips):
        head = q_ref[t, pl.ds(half, half), :]
        tail = q_ref[t, pl.ds(each, half), :]
        if t > 0:
            head = (head.astype(F32) + q_ref[t - 1, pl.ds(half + each, half), :].astype(F32)).astype(BF16)
        if t < strips - 1:
            tail = (tail.astype(F32) + q_ref[t + 1, pl.ds(0, half), :].astype(F32)).astype(BF16)
        rows += [head, q_ref[t, pl.ds(2 * half, each - 2 * half), :], tail]
    product = dot(jnp.concatenate(rows, axis=0).T, rt_ref[...]).astype(BF16)
    for a in range(out_ref.shape[0]):
        to = lax.div(owner_ref[a * sub_cols], n_strip)
        for c in range(out_ref.shape[1] // side):
            out_ref[to, pl.ds(c * side, side), :] = product[
                c * side : (c + 1) * side, a * side : (a + 1) * side
            ].T


def grid_kernel(cell_ref, dest_ref, m_ref, fr_ref, fc_ref, off_ref, grid_hbm, out_ref, g_v, s_v, o_v, count, sem):
    facets, both, side = m_ref.shape
    corr = both // side
    grid = fr_ref.shape[1]
    blocks = off_ref.shape[0]
    devices = out_ref.shape[0]

    for d in range(devices):
        count[d] = 0
    o_v[...] = jnp.zeros_like(o_v)
    copies = [pltpu.make_async_copy(g_v.at[c], grid_hbm.at[c], sem.at[c]) for c in range(corr)]
    fr = jnp.concatenate([fr_ref[f] for f in range(facets)], axis=1)
    spreads = [dot(m_ref[f], fc_ref[f], ((1,), (1,))).astype(BF16) for f in range(facets)]
    for c in range(corr):
        spread = jnp.concatenate([one_f[c * side : (c + 1) * side] for one_f in spreads], axis=0)
        sub = dot(fr, spread).astype(BF16)
        g_v[c] = sub
        copies[c].start()
        for h in range(grid // 128):
            s_v[c, h] = sub[:, h * 128 : (h + 1) * 128].astype(F32)

    lane = lax.broadcasted_iota(jnp.int32, (TILE, 128), 1)
    place = lax.broadcasted_iota(jnp.int32, (TILE, 128), 0).astype(F32)

    def weights(offset):
        delta = (place - offset) * (1.0 / KERNEL_WIDTH)
        return jnp.exp(-0.5 * delta * delta)

    def one(k):
        r, q = cell_ref[0, k], cell_ref[1, k]
        lane_tile, shift = lax.div(q, 128), lax.rem(q, 128)
        after = jnp.minimum(lane_tile + 1, grid // 128 - 1)
        tiles = []
        for c in range(corr):
            window = jnp.where(
                lane >= shift, s_v[c, lane_tile, pl.ds(r, TILE), :], s_v[c, after, pl.ds(r, TILE), :]
            )
            tiles.append(pltpu.roll(window, lax.rem(128 - shift + TILE * c, 128), 1))
        tile = tiles[0]
        for c in range(1, corr):
            tile = jnp.where(lane < TILE * c, tile, tiles[c])
        row_w = weights(off_ref[k, pl.ds(0, 1), :]).astype(BF16)
        col_w = weights(off_ref[k, pl.ds(1, 1), :])
        along = dot(tile.astype(BF16).T[: TILE * corr], row_w)
        dest = dest_ref[0, k]
        rank = count[dest]
        count[dest] = rank + 1
        values = [
            jnp.sum(along[c * TILE : (c + 1) * TILE] * col_w, axis=0, keepdims=True) for c in range(corr)
        ]
        o_v[dest, pl.ds(rank * corr, corr), :] = jnp.concatenate(values, axis=0)

    unroll = 32 if blocks % 32 == 0 else 1

    @pl.loop(0, blocks // unroll)
    def _(g):
        for u in range(unroll):
            one(g * unroll + u)

    out_ref[...] = o_v[...].astype(BF16)
    for copy in copies:
        copy.wait()


def gain_kernel(gains_ref, pair_ref, out_ref):
    corr, antennas = gains_ref.shape
    n, _, v = pair_ref.shape
    step = 32

    @pl.loop(0, n // step)
    def _(g):
        at = pl.multiple_of(g * step, step)
        product = [None] * corr
        for end in range(2):
            index = pair_ref[pl.ds(at, step), end, :]
            low = index & 127
            high = index >> 7
            for c in range(corr):
                gain = None
                for part in range(antennas // 128):
                    table = jnp.broadcast_to(gains_ref[pl.ds(c, 1), pl.ds(part * 128, 128)], (step, 128))
                    here = jnp.take_along_axis(table, low, axis=1, mode="promise_in_bounds")
                    gain = here if part == 0 else jnp.where(high == part, here, gain)
                product[c] = gain if end == 0 else product[c] * gain
        for c in range(corr):
            out_ref[pl.ds(at, step), c, :] = product[c]


VMEM = pl.BlockSpec(memory_space=pltpu.VMEM)
SMEM = pl.BlockSpec(memory_space=pltpu.SMEM)
HBM = pl.BlockSpec(memory_space=pltpu.HBM)


def residual_kernel(observed_ref, gain_ref, placed_ref, out_ref):
    out_ref[...] = observed_ref[...] - gain_ref[...] * placed_ref[...].astype(F32)


def call(kernel, name, ins, outs, shapes, scratch, mib):
    return pl.pallas_call(
        kernel,
        in_specs=ins,
        out_specs=outs,
        out_shape=shapes,
        scratch_shapes=scratch,
        compiler_params=pltpu.CompilerParams(vmem_limit_bytes=mib * 1024 * 1024),
        name=name,
    )


def in_vmem(x):
    return pltpu.with_memory_space_constraint(x, pltpu.VMEM)


def in_hbm(x):
    return pltpu.with_memory_space_constraint(x, pltpu.HBM)


def on_device(
    sky_components,
    scale_kernels,
    row_taper,
    col_taper,
    finish_rows,
    finish_cols,
    subgrid_owner,
    block_cell,
    vis_offset,
    block_owner,
    observed,
    antenna_pair_index,
    gains,
):
    n_facet = lax.axis_size("facet")
    n_strip = lax.axis_size("strip")
    devices = n_facet * n_strip
    comp = sky_components[0]
    corr, scales, rows, cols = comp.shape
    facets, grid, side = finish_cols.shape
    sub_rows = row_taper.shape[2] // side
    sub_cols = col_taper.shape[2] // side
    taps = scale_kernels.shape[1]
    out_rows = rows + taps - 1
    capacity = observed.shape[0] // devices
    visibilities = observed.shape[2]

    sent = call(
        functools.partial(column_kernel, n_strip=n_strip),
        "columns",
        [SMEM, SMEM, HBM, HBM],
        VMEM,
        pltpu.VMEM((n_strip, out_rows, corr * side), BF16),
        [
            pltpu.VMEM((corr, scales, rows, cols + 256), BF16),
            pltpu.VMEM(col_taper.shape[1:], BF16),
            pltpu.VMEM((corr, scales * rows, cols), BF16),
            pltpu.VMEM((corr * out_rows, cols), BF16),
            pltpu.SemaphoreType.DMA((4,)),
            pltpu.SemaphoreType.DMA((2,)),
        ],
        32,
    )(in_hbm(subgrid_owner), in_hbm(scale_kernels), in_hbm(comp), in_hbm(col_taper[0]))
    held = lax.all_to_all(sent, "strip", split_axis=0, concat_axis=0, tiled=True)

    parted = call(
        functools.partial(row_kernel, n_strip=n_strip, sub_cols=sub_cols),
        "rows",
        [SMEM, VMEM, VMEM],
        VMEM,
        pltpu.VMEM((n_facet, corr * side, side), BF16),
        [],
        20,
    )(subgrid_owner, in_vmem(held), in_vmem(row_taper[0]))
    mine = lax.all_to_all(parted, "facet", split_axis=0, concat_axis=0, tiled=True)

    gain = call(
        gain_kernel,
        "gain_products",
        [VMEM, VMEM],
        VMEM,
        pltpu.VMEM(observed.shape, F32),
        [],
        8,
    )(gains, antenna_pair_index)

    subgrid, outgoing = call(
        grid_kernel,
        "subgrid_and_degrid",
        [SMEM, SMEM, VMEM, VMEM, VMEM, VMEM],
        [HBM, VMEM],
        [
            jax.ShapeDtypeStruct((corr, grid, grid), BF16),
            pltpu.HBM((devices, capacity * corr, visibilities), BF16),
        ],
        [
            pltpu.VMEM((corr, grid, grid), BF16),
            pltpu.VMEM((corr, grid // 128, grid, 128), F32),
            pltpu.VMEM((devices, capacity * corr, visibilities), F32),
            pltpu.SMEM((devices,), jnp.int32),
            pltpu.SemaphoreType.DMA((corr,)),
        ],
        20,
    )(
        block_cell.T,
        block_owner.T,
        in_vmem(mine),
        in_vmem(finish_rows),
        in_vmem(finish_cols),
        in_vmem(vis_offset),
    )
    arrived = lax.all_to_all(outgoing, ("facet", "strip"), split_axis=0, concat_axis=0, tiled=True)
    merged = (devices, capacity * corr, visibilities)
    residual = call(
        residual_kernel, "residual", [VMEM, VMEM, VMEM], VMEM, jax.ShapeDtypeStruct(merged, F32), [], 8
    )(in_vmem(observed.reshape(merged)), in_vmem(gain.reshape(merged)), in_vmem(arrived))
    return (subgrid[None], residual.reshape(observed.shape))


def solution(mesh):
    placed = (
        P("facet", None, None, "strip", None),
        P(),
        P("facet", None, None),
        P("facet", None, None),
        P(),
        P(),
        P(),
        P(("facet", "strip"), None),
        P(("facet", "strip"), None, None),
        P(("facet", "strip"), None),
        P(("facet", "strip"), None, None),
        P(("facet", "strip"), None, None),
        P(),
    )
    return jax.shard_map(
        on_device,
        mesh=mesh,
        in_specs=placed,
        out_specs=(P(("facet", "strip"), None, None, None), P(("facet", "strip"), None, None)),
        check_vma=False,
    )
```

```python
import functools

import jax
import jax.numpy as jnp
from jax import lax
from jax.experimental import pallas as pl
from jax.experimental.pallas import tpu as pltpu
from jax.sharding import PartitionSpec as P

TILE = 32
KERNEL_WIDTH = 1.5
BF16 = jnp.bfloat16
F32 = jnp.float32


def dot(a, b, dims=((1,), (0,))):
    return lax.dot_general(a, b, (dims, ((), ())), preferred_element_type=F32)


def stacked(rows):
    return jnp.concatenate([jnp.concatenate(row, axis=1) for row in rows], axis=0)


def scalars(pairs, sem):
    copies = [pltpu.make_async_copy(source, to, sem.at[i]) for i, (source, to) in enumerate(pairs)]
    for copy in copies:
        copy.start()
    return copies


def circulant(kern_ref, scale, places, rows):
    lane = lax.broadcasted_iota(jnp.int32, (8, 256), 1)
    base = jnp.zeros((8, 256), F32)
    for tap, place in enumerate(places):
        base = jnp.where(lane == place % 256, kern_ref[scale, tap], base)
    return pltpu.roll(jnp.broadcast_to(base[:1], (rows, 256)), 0, 1, stride=1, stride_axis=0)


def column_kernel(
    owner_hbm, kern_hbm, x_hbm, ct_hbm, out_ref, owner_ref, kern_ref, x_v, ct_v, y_v, s_v, small_sem, x_sem, ct_sem, *, n_strip
):
    corr, scales, rows, cols = x_hbm.shape
    taps = kern_ref.shape[1]
    half = (taps - 1) // 2
    out_rows = rows + 2 * half
    side = out_ref.shape[2] // corr
    x_parts, ct_parts = x_sem.shape[0], ct_sem.shape[0]
    x_w, ct_w = cols // x_parts, cols // ct_parts
    x_copies = [
        pltpu.make_async_copy(
            x_hbm.at[:, :, :, pl.ds(x_w * m, x_w)],
            x_v.at[:, :, :, pl.ds(128 + x_w * m, x_w)],
            x_sem.at[m],
        )
        for m in range(x_parts)
    ]
    ct_copies = [
        pltpu.make_async_copy(
            ct_hbm.at[:, pl.ds(ct_w * m, ct_w)], ct_v.at[:, pl.ds(ct_w * m, ct_w)], ct_sem.at[m]
        )
        for m in range(ct_parts)
    ]
    small = scalars([(kern_hbm, kern_ref), (owner_hbm, owner_ref)], small_sem)
    for copy in x_copies:
        copy.start()
    zeros = jnp.zeros((corr, scales, rows, 128), BF16)
    x_v[:, :, :, pl.ds(0, 128)] = zeros
    x_v[:, :, :, pl.ds(128 + cols, 128)] = zeros

    for copy in small:
        copy.wait()
    columns, bands = [], []
    blank = jnp.zeros((64, 128), F32)
    zero = jnp.zeros((128, 128), BF16)
    for s in range(scales):
        wide = circulant(kern_ref, s, [half - t for t in range(taps)], 128)
        same, wrap = wide[:, :128].astype(BF16), wide[:, 128:]
        before = jnp.concatenate([blank, wrap[64:]], axis=0).astype(BF16)
        after = jnp.concatenate([wrap[:64], blank], axis=0).astype(BF16)
        columns.append(stacked([[same, before], [after, same], [before, zero], [zero, after]]))
        bands.append(circulant(kern_ref, s, [t - 2 * half for t in range(taps)], out_rows)[:, :rows].astype(BF16))
    band_all = jnp.concatenate(bands, axis=1)

    for n in range(cols // 256):
        for m in range(x_parts):
            if max(0, (x_w * m) // 256 - 1) == n:
                x_copies[m].wait()
                if m == min(1, x_parts - 1):
                    for copy in ct_copies:
                        copy.start()
        at = 128 + 256 * n
        for s in range(scales):
            mid = x_v[:, s, :, pl.ds(at, 256)].reshape(corr * rows, 256)
            before = x_v[:, s, :, pl.ds(at - 128, 128)].reshape(corr * rows, 128)
            after = x_v[:, s, :, pl.ds(at + 256, 128)].reshape(corr * rows, 128)
            y = dot(jnp.concatenate([mid, before, after], axis=1), columns[s]).astype(BF16)
            for c in range(corr):
                y_v[c, pl.ds(s * rows, rows), pl.ds(256 * n, 256)] = y[c * rows : (c + 1) * rows]
        if n % 2 == 1:
            pair = pl.ds(256 * (n - 1), 512)
            for c in range(corr):
                s_v[pl.ds(c * out_rows, out_rows), pair] = dot(band_all, y_v[c, :, pair]).astype(BF16)

    for m in range(ct_parts):
        ct_copies[m].wait()
        product = dot(s_v[...], ct_v[:, pl.ds(ct_w * m, ct_w)]).astype(BF16)
        for h in range(ct_w // side):
            to = lax.rem(owner_ref[m * (ct_w // side) + h], n_strip)
            for c in range(corr):
                out_ref[to, :, pl.ds(c * side, side)] = product[
                    c * out_rows : (c + 1) * out_rows, h * side : (h + 1) * side
                ]


def row_kernel(owner_hbm, q_ref, rt_ref, out_ref, owner_ref, small_sem, *, n_strip, sub_cols):
    (small,) = scalars([(owner_hbm, owner_ref)], small_sem)
    strips, part, _ = q_ref.shape
    each = rt_ref.shape[0] // strips
    half = (part - each) // 2
    side = out_ref.shape[2]
    rows = []
    for t in range(strips):
        head = q_ref[t, pl.ds(half, half), :]
        tail = q_ref[t, pl.ds(each, half), :]
        if t > 0:
            head = (head.astype(F32) + q_ref[t - 1, pl.ds(half + each, half), :].astype(F32)).astype(BF16)
        if t < strips - 1:
            tail = (tail.astype(F32) + q_ref[t + 1, pl.ds(0, half), :].astype(F32)).astype(BF16)
        rows += [head, q_ref[t, pl.ds(2 * half, each - 2 * half), :], tail]
    product = dot(jnp.concatenate(rows, axis=0).T, rt_ref[...]).astype(BF16)
    small.wait()
    for a in range(out_ref.shape[0]):
        to = lax.div(owner_ref[a * sub_cols], n_strip)
        for c in range(out_ref.shape[1] // side):
            out_ref[to, pl.ds(c * side, side), :] = product[
                c * side : (c + 1) * side, a * side : (a + 1) * side
            ].T


def grid_kernel(
    cell_hbm, dest_hbm, m_ref, fr_ref, fc_ref, off_ref, grid_hbm, out_ref, cell_ref, dest_ref, g_v, s_v, o_v, count, small_sem, sem
):
    small = scalars([(cell_hbm, cell_ref), (dest_hbm, dest_ref)], small_sem)
    facets, both, side = m_ref.shape
    corr = both // side
    grid = fr_ref.shape[1]
    blocks = off_ref.shape[0]
    devices = out_ref.shape[0]

    for d in range(devices):
        count[d] = 0
    o_v[...] = jnp.zeros_like(o_v)
    copies = [pltpu.make_async_copy(g_v.at[c], grid_hbm.at[c], sem.at[c]) for c in range(corr)]
    fr = jnp.concatenate([fr_ref[f] for f in range(facets)], axis=1)
    spreads = [dot(m_ref[f], fc_ref[f], ((1,), (1,))).astype(BF16) for f in range(facets)]
    for c in range(corr):
        spread = jnp.concatenate([one_f[c * side : (c + 1) * side] for one_f in spreads], axis=0)
        sub = dot(fr, spread).astype(BF16)
        g_v[c] = sub
        copies[c].start()
        for h in range(grid // 128):
            s_v[c, h] = sub[:, h * 128 : (h + 1) * 128].astype(F32)

    for copy in small:
        copy.wait()
    lane = lax.broadcasted_iota(jnp.int32, (TILE, 128), 1)
    place = lax.broadcasted_iota(jnp.int32, (TILE, 128), 0).astype(F32)

    def weights(offset):
        delta = (place - offset) * (1.0 / KERNEL_WIDTH)
        return jnp.exp(-0.5 * delta * delta)

    def one(k):
        r, q = cell_ref[0, k], cell_ref[1, k]
        lane_tile, shift = lax.div(q, 128), lax.rem(q, 128)
        after = jnp.minimum(lane_tile + 1, grid // 128 - 1)
        tiles = []
        for c in range(corr):
            window = jnp.where(
                lane >= shift, s_v[c, lane_tile, pl.ds(r, TILE), :], s_v[c, after, pl.ds(r, TILE), :]
            )
            tiles.append(pltpu.roll(window, lax.rem(128 - shift + TILE * c, 128), 1))
        tile = tiles[0]
        for c in range(1, corr):
            tile = jnp.where(lane < TILE * c, tile, tiles[c])
        row_w = weights(off_ref[k, pl.ds(0, 1), :]).astype(BF16)
        col_w = weights(off_ref[k, pl.ds(1, 1), :])
        along = dot(tile.astype(BF16).T[: TILE * corr], row_w)
        dest = dest_ref[0, k]
        rank = count[dest]
        count[dest] = rank + 1
        values = [
            jnp.sum(along[c * TILE : (c + 1) * TILE] * col_w, axis=0, keepdims=True) for c in range(corr)
        ]
        o_v[dest, pl.ds(rank * corr, corr), :] = jnp.concatenate(values, axis=0)

    unroll = 32 if blocks % 32 == 0 else 1

    @pl.loop(0, blocks // unroll)
    def _(g):
        for u in range(unroll):
            one(g * unroll + u)

    out_ref[...] = o_v[...].astype(BF16)
    for copy in copies:
        copy.wait()


def gain_kernel(gains_ref, pair_ref, out_ref):
    corr, antennas = gains_ref.shape
    n, _, v = pair_ref.shape
    step = 32

    @pl.loop(0, n // step)
    def _(g):
        at = pl.multiple_of(g * step, step)
        product = [None] * corr
        for end in range(2):
            index = pair_ref[pl.ds(at, step), end, :]
            low = index & 127
            high = index >> 7
            for c in range(corr):
                gain = None
                for part in range(antennas // 128):
                    table = jnp.broadcast_to(gains_ref[pl.ds(c, 1), pl.ds(part * 128, 128)], (step, 128))
                    here = jnp.take_along_axis(table, low, axis=1, mode="promise_in_bounds")
                    gain = here if part == 0 else jnp.where(high == part, here, gain)
                product[c] = gain if end == 0 else product[c] * gain
        for c in range(corr):
            out_ref[pl.ds(at, step), c, :] = product[c]


VMEM = pl.BlockSpec(memory_space=pltpu.VMEM)
HBM = pl.BlockSpec(memory_space=pltpu.HBM)


def residual_kernel(observed_ref, gain_ref, placed_ref, out_ref):
    out_ref[...] = observed_ref[...] - gain_ref[...] * placed_ref[...].astype(F32)


def call(kernel, name, ins, outs, shapes, scratch, mib):
    return pl.pallas_call(
        kernel,
        in_specs=ins,
        out_specs=outs,
        out_shape=shapes,
        scratch_shapes=scratch,
        compiler_params=pltpu.CompilerParams(vmem_limit_bytes=mib * 1024 * 1024),
        name=name,
    )


def in_vmem(x):
    return pltpu.with_memory_space_constraint(x, pltpu.VMEM)


def in_hbm(x):
    return pltpu.with_memory_space_constraint(x, pltpu.HBM)


def on_device(
    sky_components,
    scale_kernels,
    row_taper,
    col_taper,
    finish_rows,
    finish_cols,
    subgrid_owner,
    block_cell,
    vis_offset,
    block_owner,
    observed,
    antenna_pair_index,
    gains,
):
    n_facet = lax.axis_size("facet")
    n_strip = lax.axis_size("strip")
    devices = n_facet * n_strip
    comp = sky_components[0]
    corr, scales, rows, cols = comp.shape
    facets, grid, side = finish_cols.shape
    sub_rows = row_taper.shape[2] // side
    sub_cols = col_taper.shape[2] // side
    taps = scale_kernels.shape[1]
    out_rows = rows + taps - 1
    capacity = observed.shape[0] // devices
    visibilities = observed.shape[2]

    sent = call(
        functools.partial(column_kernel, n_strip=n_strip),
        "columns",
        [HBM, HBM, HBM, HBM],
        VMEM,
        pltpu.VMEM((n_strip, out_rows, corr * side), BF16),
        [
            pltpu.SMEM(subgrid_owner.shape, jnp.int32),
            pltpu.SMEM(scale_kernels.shape, F32),
            pltpu.VMEM((corr, scales, rows, cols + 256), BF16),
            pltpu.VMEM(col_taper.shape[1:], BF16),
            pltpu.VMEM((corr, scales * rows, cols), BF16),
            pltpu.VMEM((corr * out_rows, cols), BF16),
            pltpu.SemaphoreType.DMA((2,)),
            pltpu.SemaphoreType.DMA((4,)),
            pltpu.SemaphoreType.DMA((2,)),
        ],
        32,
    )(in_hbm(subgrid_owner), in_hbm(scale_kernels), in_hbm(comp), in_hbm(col_taper[0]))
    held = lax.all_to_all(sent, "strip", split_axis=0, concat_axis=0, tiled=True)

    parted = call(
        functools.partial(row_kernel, n_strip=n_strip, sub_cols=sub_cols),
        "rows",
        [HBM, VMEM, VMEM],
        VMEM,
        pltpu.VMEM((n_facet, corr * side, side), BF16),
        [pltpu.SMEM(subgrid_owner.shape, jnp.int32), pltpu.SemaphoreType.DMA((1,))],
        20,
    )(in_hbm(subgrid_owner), in_vmem(held), in_vmem(row_taper[0]))
    mine = lax.all_to_all(parted, "facet", split_axis=0, concat_axis=0, tiled=True)

    gain = call(
        gain_kernel,
        "gain_products",
        [VMEM, VMEM],
        VMEM,
        pltpu.VMEM(observed.shape, F32),
        [],
        8,
    )(gains, antenna_pair_index)

    subgrid, outgoing = call(
        grid_kernel,
        "subgrid_and_degrid",
        [HBM, HBM, VMEM, VMEM, VMEM, VMEM],
        [HBM, VMEM],
        [
            jax.ShapeDtypeStruct((corr, grid, grid), BF16),
            pltpu.HBM((devices, capacity * corr, visibilities), BF16),
        ],
        [
            pltpu.SMEM(block_cell.shape[::-1], jnp.int32),
            pltpu.SMEM(block_owner.shape[::-1], jnp.int32),
            pltpu.VMEM((corr, grid, grid), BF16),
            pltpu.VMEM((corr, grid // 128, grid, 128), F32),
            pltpu.VMEM((devices, capacity * corr, visibilities), F32),
            pltpu.SMEM((devices,), jnp.int32),
            pltpu.SemaphoreType.DMA((2,)),
            pltpu.SemaphoreType.DMA((corr,)),
        ],
        20,
    )(
        in_hbm(block_cell.T),
        in_hbm(block_owner.T),
        in_vmem(mine),
        in_vmem(finish_rows),
        in_vmem(finish_cols),
        in_vmem(vis_offset),
    )
    arrived = lax.all_to_all(outgoing, ("facet", "strip"), split_axis=0, concat_axis=0, tiled=True)
    merged = (devices, capacity * corr, visibilities)
    residual = call(
        residual_kernel, "residual", [VMEM, VMEM, VMEM], VMEM, jax.ShapeDtypeStruct(merged, F32), [], 8
    )(in_vmem(observed.reshape(merged)), in_vmem(gain.reshape(merged)), in_vmem(arrived))
    return (subgrid[None], residual.reshape(observed.shape))


def solution(mesh):
    placed = (
        P("facet", None, None, "strip", None),
        P(),
        P("facet", None, None),
        P("facet", None, None),
        P(),
        P(),
        P(),
        P(("facet", "strip"), None),
        P(("facet", "strip"), None, None),
        P(("facet", "strip"), None),
        P(("facet", "strip"), None, None),
        P(("facet", "strip"), None, None),
        P(),
    )
    return jax.shard_map(
        on_device,
        mesh=mesh,
        in_specs=placed,
        out_specs=(P(("facet", "strip"), None, None, None), P(("facet", "strip"), None, None)),
        check_vma=False,
    )
```

```python
import functools

import jax
import jax.numpy as jnp
from jax import lax
from jax.experimental import pallas as pl
from jax.experimental.pallas import tpu as pltpu
from jax.sharding import PartitionSpec as P

TILE = 32
KERNEL_WIDTH = 1.5
BF16 = jnp.bfloat16
F32 = jnp.float32


def dot(a, b, dims=((1,), (0,))):
    return lax.dot_general(a, b, (dims, ((), ())), preferred_element_type=F32)


def stacked(rows):
    return jnp.concatenate([jnp.concatenate(row, axis=1) for row in rows], axis=0)


def scalars(pairs, sem):
    copies = [pltpu.make_async_copy(source, to, sem.at[i]) for i, (source, to) in enumerate(pairs)]
    for copy in copies:
        copy.start()
    return copies


def circulant(kern_ref, scale, places, rows):
    lane = lax.broadcasted_iota(jnp.int32, (8, 256), 1)
    base = jnp.zeros((8, 256), F32)
    for tap, place in enumerate(places):
        base = jnp.where(lane == place % 256, kern_ref[scale, tap], base)
    return pltpu.roll(jnp.broadcast_to(base[:1], (rows, 256)), 0, 1, stride=1, stride_axis=0)


def column_kernel(
    owner_hbm, kern_hbm, x_hbm, ct_hbm, out_ref, owner_ref, kern_ref, x_v, ct_v, y_v, s_v, small_sem, x_sem, ct_sem, *, n_strip
):
    corr, scales, rows, cols = x_hbm.shape
    taps = kern_ref.shape[1]
    half = (taps - 1) // 2
    out_rows = rows + 2 * half
    side = out_ref.shape[2] // corr
    x_parts, ct_parts = x_sem.shape[0], ct_sem.shape[0]
    x_w, ct_w = cols // x_parts, cols // ct_parts
    x_copies = [
        pltpu.make_async_copy(
            x_hbm.at[:, :, :, pl.ds(x_w * m, x_w)],
            x_v.at[:, :, :, pl.ds(128 + x_w * m, x_w)],
            x_sem.at[m],
        )
        for m in range(x_parts)
    ]
    ct_copies = [
        pltpu.make_async_copy(
            ct_hbm.at[:, pl.ds(ct_w * m, ct_w)], ct_v.at[:, pl.ds(ct_w * m, ct_w)], ct_sem.at[m]
        )
        for m in range(ct_parts)
    ]
    small = scalars([(kern_hbm, kern_ref), (owner_hbm, owner_ref)], small_sem)
    for copy in x_copies:
        copy.start()
    zeros = jnp.zeros((corr, scales, rows, 128), BF16)
    x_v[:, :, :, pl.ds(0, 128)] = zeros
    x_v[:, :, :, pl.ds(128 + cols, 128)] = zeros

    for copy in small:
        copy.wait()
    columns, bands = [], []
    blank = jnp.zeros((64, 128), F32)
    zero = jnp.zeros((128, 128), BF16)
    for s in range(scales):
        wide = circulant(kern_ref, s, [half - t for t in range(taps)], 128)
        same, wrap = wide[:, :128].astype(BF16), wide[:, 128:]
        before = jnp.concatenate([blank, wrap[64:]], axis=0).astype(BF16)
        after = jnp.concatenate([wrap[:64], blank], axis=0).astype(BF16)
        columns.append(stacked([[same, before], [after, same], [before, zero], [zero, after]]))
        bands.append(circulant(kern_ref, s, [t - 2 * half for t in range(taps)], out_rows)[:, :rows].astype(BF16))
    band_all = jnp.concatenate(bands, axis=1)

    for n in range(cols // 256):
        for m in range(x_parts):
            if max(0, (x_w * m) // 256 - 1) == n:
                x_copies[m].wait()
                if m == min(1, x_parts - 1):
                    for copy in ct_copies:
                        copy.start()
        at = 128 + 256 * n
        for s in range(scales):
            mid = x_v[:, s, :, pl.ds(at, 256)].reshape(corr * rows, 256)
            before = x_v[:, s, :, pl.ds(at - 128, 128)].reshape(corr * rows, 128)
            after = x_v[:, s, :, pl.ds(at + 256, 128)].reshape(corr * rows, 128)
            y = dot(jnp.concatenate([mid, before, after], axis=1), columns[s]).astype(BF16)
            for c in range(corr):
                to = 256 * (2 * corr * (n // 2) + 2 * c + n % 2)
                y_v[pl.ds(s * rows, rows), pl.ds(to, 256)] = y[c * rows : (c + 1) * rows]
        if n % 2 == 2 - 1:
            first = 256 * (n - 2 + 1)
            smooth = dot(band_all, y_v[:, pl.ds(corr * first, corr * 256 * 2)]).astype(BF16)
            for c in range(corr):
                s_v[pl.ds(c * out_rows, out_rows), pl.ds(first, 256 * 2)] = smooth[:, c * 256 * 2 : (c + 1) * 256 * 2]

    for m in range(ct_parts):
        ct_copies[m].wait()
        product = dot(s_v[...], ct_v[:, pl.ds(ct_w * m, ct_w)]).astype(BF16)
        for h in range(ct_w // side):
            to = lax.rem(owner_ref[m * (ct_w // side) + h], n_strip)
            for c in range(corr):
                out_ref[to, :, pl.ds(c * side, side)] = product[
                    c * out_rows : (c + 1) * out_rows, h * side : (h + 1) * side
                ]


def row_kernel(owner_hbm, q_ref, rt_ref, out_ref, owner_ref, small_sem, *, n_strip, sub_cols):
    (small,) = scalars([(owner_hbm, owner_ref)], small_sem)
    strips, part, _ = q_ref.shape
    each = rt_ref.shape[0] // strips
    half = (part - each) // 2
    side = out_ref.shape[2]
    rows = []
    for t in range(strips):
        head = q_ref[t, pl.ds(half, half), :]
        tail = q_ref[t, pl.ds(each, half), :]
        if t > 0:
            head = (head.astype(F32) + q_ref[t - 1, pl.ds(half + each, half), :].astype(F32)).astype(BF16)
        if t < strips - 1:
            tail = (tail.astype(F32) + q_ref[t + 1, pl.ds(0, half), :].astype(F32)).astype(BF16)
        rows += [head, q_ref[t, pl.ds(2 * half, each - 2 * half), :], tail]
    product = dot(jnp.concatenate(rows, axis=0).T, rt_ref[...]).astype(BF16)
    small.wait()
    for a in range(out_ref.shape[0]):
        to = lax.div(owner_ref[a * sub_cols], n_strip)
        for c in range(out_ref.shape[1] // side):
            out_ref[to, pl.ds(c * side, side), :] = product[
                c * side : (c + 1) * side, a * side : (a + 1) * side
            ].T


def grid_kernel(
    cell_hbm, dest_hbm, m_ref, fr_ref, fc_ref, off_ref, grid_hbm, out_ref, cell_ref, dest_ref, g_v, s_v, o_v, count, small_sem, sem
):
    small = scalars([(cell_hbm, cell_ref), (dest_hbm, dest_ref)], small_sem)
    facets, both, side = m_ref.shape
    corr = both // side
    grid = fr_ref.shape[1]
    blocks = off_ref.shape[0]
    devices = out_ref.shape[0]

    for d in range(devices):
        count[d] = 0
    o_v[...] = jnp.zeros_like(o_v)
    copies = [pltpu.make_async_copy(g_v.at[c], grid_hbm.at[c], sem.at[c]) for c in range(corr)]
    fr = jnp.concatenate([fr_ref[f] for f in range(facets)], axis=1)
    spreads = [dot(m_ref[f], fc_ref[f], ((1,), (1,))).astype(BF16) for f in range(facets)]
    for c in range(corr):
        spread = jnp.concatenate([one_f[c * side : (c + 1) * side] for one_f in spreads], axis=0)
        sub = dot(fr, spread).astype(BF16)
        g_v[c] = sub
        copies[c].start()
        for h in range(grid // 128):
            s_v[c, h] = sub[:, h * 128 : (h + 1) * 128].astype(F32)

    for copy in small:
        copy.wait()
    lane = lax.broadcasted_iota(jnp.int32, (TILE, 128), 1)
    place = lax.broadcasted_iota(jnp.int32, (TILE, 128), 0).astype(F32)

    def weights(offset):
        delta = (place - offset) * (1.0 / KERNEL_WIDTH)
        return jnp.exp(-0.5 * delta * delta)

    def one(k):
        r, q = cell_ref[0, k], cell_ref[1, k]
        lane_tile, shift = lax.div(q, 128), lax.rem(q, 128)
        after = jnp.minimum(lane_tile + 1, grid // 128 - 1)
        tiles = []
        for c in range(corr):
            window = jnp.where(
                lane >= shift, s_v[c, lane_tile, pl.ds(r, TILE), :], s_v[c, after, pl.ds(r, TILE), :]
            )
            tiles.append(pltpu.roll(window, lax.rem(128 - shift + TILE * c, 128), 1))
        tile = tiles[0]
        for c in range(1, corr):
            tile = jnp.where(lane < TILE * c, tile, tiles[c])
        row_w = weights(off_ref[k, pl.ds(0, 1), :]).astype(BF16)
        col_w = weights(off_ref[k, pl.ds(1, 1), :])
        along = dot(tile.astype(BF16).T[: TILE * corr], row_w)
        dest = dest_ref[0, k]
        rank = count[dest]
        count[dest] = rank + 1
        values = [
            jnp.sum(along[c * TILE : (c + 1) * TILE] * col_w, axis=0, keepdims=True) for c in range(corr)
        ]
        o_v[dest, pl.ds(rank * corr, corr), :] = jnp.concatenate(values, axis=0)

    unroll = 32 if blocks % 32 == 0 else 1

    @pl.loop(0, blocks // unroll)
    def _(g):
        for u in range(unroll):
            one(g * unroll + u)

    out_ref[...] = o_v[...].astype(BF16)
    for copy in copies:
        copy.wait()


def gain_kernel(gains_ref, pair_ref, out_ref):
    corr, antennas = gains_ref.shape
    n, _, v = pair_ref.shape
    step = 32

    @pl.loop(0, n // step)
    def _(g):
        at = pl.multiple_of(g * step, step)
        product = [None] * corr
        for end in range(2):
            index = pair_ref[pl.ds(at, step), end, :]
            low = index & 127
            high = index >> 7
            for c in range(corr):
                gain = None
                for part in range(antennas // 128):
                    table = jnp.broadcast_to(gains_ref[pl.ds(c, 1), pl.ds(part * 128, 128)], (step, 128))
                    here = jnp.take_along_axis(table, low, axis=1, mode="promise_in_bounds")
                    gain = here if part == 0 else jnp.where(high == part, here, gain)
                product[c] = gain if end == 0 else product[c] * gain
        for c in range(corr):
            out_ref[pl.ds(at, step), c, :] = product[c]


VMEM = pl.BlockSpec(memory_space=pltpu.VMEM)
HBM = pl.BlockSpec(memory_space=pltpu.HBM)


def residual_kernel(observed_ref, gain_ref, placed_ref, out_hbm, out_v, sem):
    parts = sem.shape[0]
    each = out_v.shape[0] // parts
    copies = []
    for m in range(parts):
        part = pl.ds(each * m, each)
        out_v[part] = observed_ref[part] - gain_ref[part] * placed_ref[part].astype(F32)
        copies.append(pltpu.make_async_copy(out_v.at[part], out_hbm.at[part], sem.at[m]))
        copies[m].start()
    for copy in copies:
        copy.wait()


def call(kernel, name, ins, outs, shapes, scratch, mib):
    return pl.pallas_call(
        kernel,
        in_specs=ins,
        out_specs=outs,
        out_shape=shapes,
        scratch_shapes=scratch,
        compiler_params=pltpu.CompilerParams(vmem_limit_bytes=mib * 1024 * 1024),
        name=name,
    )


def in_vmem(x):
    return pltpu.with_memory_space_constraint(x, pltpu.VMEM)


def in_hbm(x):
    return pltpu.with_memory_space_constraint(x, pltpu.HBM)


def on_device(
    sky_components,
    scale_kernels,
    row_taper,
    col_taper,
    finish_rows,
    finish_cols,
    subgrid_owner,
    block_cell,
    vis_offset,
    block_owner,
    observed,
    antenna_pair_index,
    gains,
):
    n_facet = lax.axis_size("facet")
    n_strip = lax.axis_size("strip")
    devices = n_facet * n_strip
    comp = sky_components[0]
    corr, scales, rows, cols = comp.shape
    facets, grid, side = finish_cols.shape
    sub_rows = row_taper.shape[2] // side
    sub_cols = col_taper.shape[2] // side
    taps = scale_kernels.shape[1]
    out_rows = rows + taps - 1
    capacity = observed.shape[0] // devices
    visibilities = observed.shape[2]

    sent = call(
        functools.partial(column_kernel, n_strip=n_strip),
        "columns",
        [HBM, HBM, HBM, HBM],
        VMEM,
        pltpu.VMEM((n_strip, out_rows, corr * side), BF16),
        [
            pltpu.SMEM(subgrid_owner.shape, jnp.int32),
            pltpu.SMEM(scale_kernels.shape, F32),
            pltpu.VMEM((corr, scales, rows, cols + 256), BF16),
            pltpu.VMEM(col_taper.shape[1:], BF16),
            pltpu.VMEM((scales * rows, corr * cols), BF16),
            pltpu.VMEM((corr * out_rows, cols), BF16),
            pltpu.SemaphoreType.DMA((2,)),
            pltpu.SemaphoreType.DMA((4,)),
            pltpu.SemaphoreType.DMA((2,)),
        ],
        32,
    )(in_hbm(subgrid_owner), in_hbm(scale_kernels), in_hbm(comp), in_hbm(col_taper[0]))
    held = lax.all_to_all(sent, "strip", split_axis=0, concat_axis=0, tiled=True)

    parted = call(
        functools.partial(row_kernel, n_strip=n_strip, sub_cols=sub_cols),
        "rows",
        [HBM, VMEM, VMEM],
        VMEM,
        pltpu.VMEM((n_facet, corr * side, side), BF16),
        [pltpu.SMEM(subgrid_owner.shape, jnp.int32), pltpu.SemaphoreType.DMA((1,))],
        20,
    )(in_hbm(subgrid_owner), in_vmem(held), in_vmem(row_taper[0]))
    mine = lax.all_to_all(parted, "facet", split_axis=0, concat_axis=0, tiled=True)

    gain = call(
        gain_kernel,
        "gain_products",
        [VMEM, VMEM],
        VMEM,
        pltpu.VMEM(observed.shape, F32),
        [],
        8,
    )(gains, antenna_pair_index)

    subgrid, outgoing = call(
        grid_kernel,
        "subgrid_and_degrid",
        [HBM, HBM, VMEM, VMEM, VMEM, VMEM],
        [HBM, VMEM],
        [
            jax.ShapeDtypeStruct((corr, grid, grid), BF16),
            pltpu.HBM((devices, capacity * corr, visibilities), BF16),
        ],
        [
            pltpu.SMEM(block_cell.shape[::-1], jnp.int32),
            pltpu.SMEM(block_owner.shape[::-1], jnp.int32),
            pltpu.VMEM((corr, grid, grid), BF16),
            pltpu.VMEM((corr, grid // 128, grid, 128), F32),
            pltpu.VMEM((devices, capacity * corr, visibilities), F32),
            pltpu.SMEM((devices,), jnp.int32),
            pltpu.SemaphoreType.DMA((2,)),
            pltpu.SemaphoreType.DMA((corr,)),
        ],
        20,
    )(
        in_hbm(block_cell.T),
        in_hbm(block_owner.T),
        in_vmem(mine),
        in_vmem(finish_rows),
        in_vmem(finish_cols),
        in_vmem(vis_offset),
    )
    arrived = lax.all_to_all(outgoing, ("facet", "strip"), split_axis=0, concat_axis=0, tiled=True)
    merged = (devices, capacity * corr, visibilities)
    residual = call(
        residual_kernel,
        "residual",
        [VMEM, VMEM, VMEM],
        HBM,
        jax.ShapeDtypeStruct(merged, F32),
        [pltpu.VMEM(merged, F32), pltpu.SemaphoreType.DMA((4,))],
        8,
    )(in_vmem(observed.reshape(merged)), in_vmem(gain.reshape(merged)), in_vmem(arrived))
    return (subgrid[None], residual.reshape(observed.shape))


def solution(mesh):
    placed = (
        P("facet", None, None, "strip", None),
        P(),
        P("facet", None, None),
        P("facet", None, None),
        P(),
        P(),
        P(),
        P(("facet", "strip"), None),
        P(("facet", "strip"), None, None),
        P(("facet", "strip"), None),
        P(("facet", "strip"), None, None),
        P(("facet", "strip"), None, None),
        P(),
    )
    return jax.shard_map(
        on_device,
        mesh=mesh,
        in_specs=placed,
        out_specs=(P(("facet", "strip"), None, None, None), P(("facet", "strip"), None, None)),
        check_vma=False,
    )
```
